128 devices in a mesh: row: 8 (over x, core), col: 16 (over z, y).
Axes of the slice: x: 4, y: 4, z: 4, core: 2. Of those that a mesh axis runs over, the one named last changes fastest.
Arguments:
- tile_weight: bfloat16 [128, 128, 2, 128, 128], P(('row', 'col')), may hold values from 0.049804688 to 1
- tile_angle: bfloat16 [128, 128, 2, 128, 128], P(('row', 'col')), may hold values from -3.140625 to 3.140625
- tile_list: int32 [128, 128, 2, 2], P(('row', 'col')), may hold values from 0 to 255, as said below
- tile_count: int32 [128, 128], P(('row', 'col')), may hold values from 0 to 2, as said below
- init_basis: float32 [2, 32, 32768], P(None, None, ('row', 'col')), may hold values from -6 to 6
Outputs:
- basis: float32 [2, 32, 32768], P(None, None, ('row', 'col'))
The draws below stay inside these ranges and needn't reach their ends.
Inputs may be any that keep to these rules, and one draw needn't show every extreme that they name: `tile_list`: let piece(b) = b // 2 for a block b, and number devices s = a * 16 + e' along row+col. For device s = a * 16 + b' and destination d = f * 16 + e, slot [s, d, k] holds I with piece(I) = a * 16 + e and J with piece(J) = f * 16 + b'. The slots of one s, d hold distinct tiles; for d = s they hold the diagonal tiles (I, I) of the first 2 blocks of the device's piece. tile_count[s, s] = 2, and one destination has 2 live slots from every device.
All inputs are finite; a program needn't handle non-finite values.
Results may differ from the reference program's by a relative error of at most 0.0053.
Values may be sent and summed in bfloat16 or wider, within the bound.
No kernel may reach another device: no remote copies, remote signals or barrier semaphores. Data moves between devices by JAX's collectives and lax.ppermute only.
A program may use at most 256 MiB of HBM per device.

```python
import math
import jax
import jax.numpy as jnp
from jax import lax

TILE = 128
BASIS = 32
BLK_DEV = 2
PAIR_CAP = 2
ITERS = 3
GRID_COLS = 16
IMAGES = 32768
DEVICES = 128


def draw_tile_list(key, part):
    source = jnp.arange(DEVICES)[:, None]
    target = jnp.arange(DEVICES)[None, :]
    src_row = source // GRID_COLS
    src_col = source % GRID_COLS
    dst_row = target // GRID_COLS
    dst_col = target % GRID_COLS
    piece_rows = src_row * GRID_COLS + dst_col
    segment_columns = dst_row * GRID_COLS + src_col
    combos = BLK_DEV * BLK_DEV
    scores = jax.random.randint(jax.random.fold_in(key, 11), (DEVICES, DEVICES, combos), 0, 1 << 20) * combos + jnp.arange(combos)[None, None, :]
    order = jnp.argsort(scores, axis=-1)[:, :, :PAIR_CAP]
    offset_row = order // BLK_DEV
    offset_col = order % BLK_DEV
    same = (source == target)[:, :, None]
    slots = jnp.arange(PAIR_CAP)[None, None, :]
    offset_row = jnp.where(same, slots, offset_row)
    offset_col = jnp.where(same, slots, offset_col)
    rows = piece_rows[:, :, None] * BLK_DEV + offset_row
    cols = segment_columns[:, :, None] * BLK_DEV + offset_col
    return jnp.stack([rows, cols], -1).astype(jnp.int32)


def draw_tile_count(key, part):
    counts = jax.random.randint(jax.random.fold_in(key, 21), (DEVICES, DEVICES), 0, PAIR_CAP + 1)
    busiest = jax.random.randint(jax.random.fold_in(key, 22), (), 0, DEVICES)
    places = jnp.arange(DEVICES)
    full = (places[None, :] == busiest) | (places[:, None] == places[None, :])
    return jnp.where(full, PAIR_CAP, counts).astype(jnp.int32)


def shard_levels(key, extent, split, smallest, top_value):
    def one(axis_at, shards_of):
        heights = jax.random.uniform(jax.random.fold_in(jax.random.fold_in(key, 6), axis_at), (shards_of,), jnp.float32, smallest / len(split), top_value / len(split))
        return jnp.repeat(jnp.exp(heights), extent[axis_at] // shards_of).reshape((-1,) + (1,) * (len(extent) - axis_at - 1))

    gain = one(*split[0])
    for cut in split[1:]:
        gain = gain * one(*cut)
    return gain


def gaussian(key, extent, spread, most, shards=(), held_as=jnp.bfloat16):
    values = spread * jax.random.normal(key, extent, jnp.float32)
    if shards:
        values = values * shard_levels(key, extent, shards, -0.22, 0.18)
    return jnp.clip(values, -most, most).astype(held_as)


def setup_inputs(seed: int = 0) -> dict:
    arg_keys = jax.random.split(jax.random.key(seed), 6)
    return {
        "tile_weight": jnp.clip(jnp.exp(math.log(1.0) - 2.9996462 * jax.random.uniform(arg_keys[0], (DEVICES, DEVICES, PAIR_CAP, TILE, TILE), jnp.float32) ** shard_levels(arg_keys[0], (DEVICES, DEVICES, PAIR_CAP, TILE, TILE), ((0, 128),), -0.2, 0.2)), 0.049804688, 1.0).astype(jnp.bfloat16),
        "tile_angle": jnp.clip(jax.random.uniform(arg_keys[1], (DEVICES, DEVICES, PAIR_CAP, TILE, TILE), jnp.float32, -3.140625, 3.140625), -3.140625, 3.140625).astype(jnp.bfloat16),
        "tile_list": draw_tile_list(jax.random.fold_in(arg_keys[5], 71), 0),
        "tile_count": draw_tile_count(jax.random.fold_in(arg_keys[5], 71), 0),
        "init_basis": gaussian(arg_keys[4], (2, BASIS, IMAGES), 1.0, 6.0, ((2, 128),), jnp.float32),
    }


def complex_tiles(weight, angle):
    weight_f = weight.astype(jnp.float32)
    angle_f = angle.astype(jnp.float32)
    return ((weight_f * jnp.cos(angle_f)).astype(jnp.bfloat16), (weight_f * jnp.sin(angle_f)).astype(jnp.bfloat16))

def highest_dot(left, right):
    return jnp.dot(left, right, precision=lax.Precision.HIGHEST, preferred_element_type=jnp.float32)

def gram_terms(image_real, image_imag):
    gram_real = highest_dot(image_real, image_real.T) + highest_dot(image_imag, image_imag.T)
    gram_imag = highest_dot(image_real, image_imag.T) - highest_dot(image_imag, image_real.T)
    return (gram_real, gram_imag)

def orthonormal(gram_real, gram_imag, image_real, image_imag):
    width = gram_real.shape[0]
    indices = jnp.arange(width)
    ridge = 0.01 * jnp.trace(gram_real) / width + 1e-06
    gram_real = gram_real + ridge * jnp.eye(width, dtype=jnp.float32)
    lower_real = jnp.zeros((width, width), jnp.float32)
    lower_imag = jnp.zeros((width, width), jnp.float32)
    for column in range(width):
        prod_real = highest_dot(lower_real, lower_real[column]) + highest_dot(lower_imag, lower_imag[column])
        prod_imag = highest_dot(lower_imag, lower_real[column]) - highest_dot(lower_real, lower_imag[column])
        pivot = jnp.sqrt(gram_real[column, column] - prod_real[column])
        below = indices > column
        col_real = (gram_real[:, column] - prod_real) / pivot
        col_imag = (gram_imag[:, column] - prod_imag) / pivot
        lower_real = lower_real.at[:, column].set(jnp.where(below, col_real, jnp.where(indices == column, pivot, 0.0)))
        lower_imag = lower_imag.at[:, column].set(jnp.where(below, col_imag, 0.0))
    inv_real = jnp.zeros((width, width), jnp.float32)
    inv_imag = jnp.zeros((width, width), jnp.float32)
    for column in range(width):
        unit = (indices == column).astype(jnp.float32)
        sum_real = highest_dot(lower_real[column], inv_real) - highest_dot(lower_imag[column], inv_imag)
        sum_imag = highest_dot(lower_real[column], inv_imag) + highest_dot(lower_imag[column], inv_real)
        diag_value = lower_real[column, column]
        inv_real = inv_real.at[column].set((unit - sum_real) / diag_value)
        inv_imag = inv_imag.at[column].set(-sum_imag / diag_value)
    new_real = highest_dot(inv_real, image_real) + highest_dot(inv_imag, image_imag)
    new_imag = highest_dot(inv_real, image_imag) - highest_dot(inv_imag, image_real)
    return jnp.stack([new_real, new_imag], 0)

def reference(tile_weight, tile_angle, tile_list, tile_count, init_basis):
    blocks_all = IMAGES // TILE
    slot_count = DEVICES * PAIR_CAP
    listing = tile_list.reshape(DEVICES, slot_count, 2).astype(jnp.int32)
    alive = (jnp.arange(PAIR_CAP)[None, None, :] < tile_count[:, :, None]).reshape(DEVICES, slot_count)
    halves = jnp.where(alive, 0.5, 0.0).astype(jnp.float32)
    weights = tile_weight.reshape(DEVICES, slot_count, TILE, TILE)
    angles = tile_angle.reshape(DEVICES, slot_count, TILE, TILE)

    def degree_step(carry, item):
        weight, pairs, half_w = item
        row_sums = lax.optimization_barrier(jnp.sum(weight.astype(jnp.float32), axis=2))
        col_sums = lax.optimization_barrier(jnp.sum(weight.astype(jnp.float32), axis=1))
        carry = carry.at[pairs[:, 0]].add(half_w[:, None] * row_sums)
        carry = carry.at[pairs[:, 1]].add(half_w[:, None] * col_sums)
        return (carry, None)
    degree, _ = lax.scan(degree_step, jnp.zeros((blocks_all, TILE), jnp.float32), (weights, listing, halves))
    scale = lax.rsqrt(degree)
    basis = init_basis.astype(jnp.float32)
    for rounds in range(ITERS):
        scaled = (basis.reshape(2, BASIS, blocks_all, TILE) * scale[None, None]).astype(jnp.bfloat16)
        blocks = jnp.transpose(scaled, (2, 0, 1, 3))

        def apply_step(carry, item):
            weight, angle, pairs, half_w = item
            real_part, imag_part = complex_tiles(weight, angle)
            real_factor = real_part.astype(jnp.float32)
            imaginary_factor = imag_part.astype(jnp.float32)
            from_cols = blocks[pairs[:, 1]].astype(jnp.float32)
            source_row_blocks = blocks[pairs[:, 0]].astype(jnp.float32)
            fwd_a = jnp.einsum('nskj,nij->nski', from_cols, real_factor)
            fwd_b = jnp.einsum('nskj,nij->nski', from_cols, imaginary_factor)
            forward = jnp.stack([fwd_a[:, 0] - fwd_b[:, 1], fwd_a[:, 1] + fwd_b[:, 0]], 1)
            reflected_first = jnp.einsum('chqr,crg->chqg', source_row_blocks, real_factor)
            reflected_second = jnp.einsum('chqr,crg->chqg', source_row_blocks, imaginary_factor)
            reflected_tile = jnp.stack([reflected_first[:, 0] + reflected_second[:, 1], reflected_first[:, 1] - reflected_second[:, 0]], 1)
            carry = carry.at[pairs[:, 0]].add(half_w[:, None, None, None] * forward)
            carry = carry.at[pairs[:, 1]].add(half_w[:, None, None, None] * reflected_tile)
            return (carry, None)
        image, _ = lax.scan(apply_step, jnp.zeros((blocks_all, 2, BASIS, TILE), jnp.float32), (weights, angles, listing, halves))
        image = image * scale[:, None, None, :]
        image = jnp.transpose(image, (1, 2, 0, 3)).reshape(2, BASIS, IMAGES)
        gram_real, gram_imag = gram_terms(image[0], image[1])
        basis = orthonormal(gram_real / IMAGES, gram_imag / IMAGES, image[0], image[1])
    return basis
```

```python
import functools

import jax
import jax.numpy as jnp
from jax import lax
from jax.experimental import pallas as pl
from jax.experimental.pallas import tpu as pltpu
from jax.sharding import PartitionSpec as P

ITERS = 3
IMAGES = 32768
TILE = 128
WIDTH = 32
SLOTS = 256
ROW_BLOCKS = 32
COL_BLOCKS = 16
CHUNK = 16
TRIG_CHUNK = 8
HALF_SIN = (0.5, -0.020833322778344154, 0.00026040783268399537, -1.5475804957532091e-06, 5.088141019626846e-09)
HALF_COS = (0.9999999403953552, -0.1249997615814209, 0.0026039734948426485, -2.164632678613998e-05, 9.044046578310372e-08)
HIGHEST = lax.Precision.HIGHEST
MIB = 1 << 20


def horner(u, coefs):
    value = coefs[-1]
    for coef in coefs[-2::-1]:
        value = value * u + coef
    return value


def lanes(shape):
    return lax.broadcasted_iota(jnp.int32, shape, 1)


def pair_swap(x):
    even = (lanes(x.shape) // WIDTH) % 2 == 0
    return jnp.where(even, -pltpu.roll(x, TILE - WIDTH, 1), pltpu.roll(x, WIDTH, 1))


def degree_kernel(rows_of, cols_of, live, w_ref, row_ref, col_ref, row_acc, col_acc):
    step = pl.program_id(0)

    @pl.when(step == 0)
    def _():
        row_acc[...] = jnp.zeros_like(row_acc)
        col_acc[...] = jnp.zeros_like(col_acc)

    for u in range(CHUNK):
        slot = step * CHUNK + u

        @pl.when(live[slot] > 0)
        def _():
            w = w_ref[u].astype(jnp.float32)
            row_acc[rows_of[slot]] += w
            col_acc[cols_of[slot]] += jnp.sum(w.reshape(TILE // 8, 8, TILE), axis=0)

    @pl.when(step == SLOTS // CHUNK - 1)
    def _():
        for p in range(ROW_BLOCKS // 2):
            sums = [jnp.sum(row_acc[2 * p + k].T, axis=0, keepdims=True) for k in range(2)]
            row_ref[p] = 0.5 * jnp.concatenate(sums * 4, axis=0)
        for p in range(COL_BLOCKS // 2):
            sums = [jnp.sum(col_acc[2 * p + k], axis=0, keepdims=True) for k in range(2)]
            col_ref[p] = 0.5 * jnp.concatenate(sums * 4, axis=0)


def degrees(rows_of, cols_of, live, weights):
    return pl.pallas_call(
        degree_kernel,
        grid_spec=pltpu.PrefetchScalarGridSpec(
            num_scalar_prefetch=3,
            grid=(SLOTS // CHUNK,),
            in_specs=[pl.BlockSpec((CHUNK, TILE, TILE), lambda c, *_: (c, 0, 0))],
            out_specs=[
                pl.BlockSpec((ROW_BLOCKS // 2, 8, TILE), lambda c, *_: (0, 0, 0)),
                pl.BlockSpec((COL_BLOCKS // 2, 8, TILE), lambda c, *_: (0, 0, 0)),
            ],
            scratch_shapes=[
                pltpu.VMEM((ROW_BLOCKS, TILE, TILE), jnp.float32),
                pltpu.VMEM((COL_BLOCKS, 8, TILE), jnp.float32),
            ],
        ),
        out_shape=[
            jax.ShapeDtypeStruct((ROW_BLOCKS // 2, 8, TILE), jnp.float32),
            jax.ShapeDtypeStruct((COL_BLOCKS // 2, 8, TILE), jnp.float32),
        ],
        compiler_params=pltpu.CompilerParams(vmem_limit_bytes=16 * MIB),
        cost_estimate=pl.CostEstimate(flops=0, bytes_accessed=18 * MIB, transcendentals=0),
        name="degrees",
    )(rows_of, cols_of, live, weights)


def tiles_kernel(order, count, *refs):
    w_refs, a_refs = refs[:TRIG_CHUNK], refs[TRIG_CHUNK : 2 * TRIG_CHUNK]
    plain_ref, turned_ref = refs[2 * TRIG_CHUNK :]
    step = pl.program_id(0)

    @pl.when(step * TRIG_CHUNK < pl.cdiv(count[0], CHUNK) * CHUNK)
    def _():
        for u in range(TRIG_CHUNK):
            half = jnp.where(step * TRIG_CHUNK + u < count[0], 0.5, 0.0).astype(jnp.float32)
            theta = a_refs[u][0].astype(jnp.float32)
            w = w_refs[u][0].astype(jnp.float32) * half
            square = theta * theta
            sine = theta * horner(square, HALF_SIN)
            cosine = horner(square, HALF_COS)
            part = (w + w) * sine
            real = w - part * sine
            imag = part * cosine
            plain_ref[u, :, :TILE] = real.astype(jnp.bfloat16)
            plain_ref[u, :, TILE:] = imag.astype(jnp.bfloat16)
            turned_ref[u, :, :TILE] = real.T.astype(jnp.bfloat16)
            turned_ref[u, :, TILE:] = imag.T.astype(jnp.bfloat16)


def complex_tiles(order, count, weights, angles):
    steps = SLOTS // TRIG_CHUNK

    def last(count):
        return pl.cdiv(count[0], CHUNK) * (CHUNK // TRIG_CHUNK) - 1

    def taken(u):
        return pl.BlockSpec(
            (1, TILE, TILE),
            lambda c, order, count: (order[jnp.minimum(c, last(count)) * TRIG_CHUNK + u], 0, 0),
        )

    out = pl.BlockSpec(
        (TRIG_CHUNK, TILE, 2 * TILE), lambda c, order, count: (jnp.minimum(c, last(count)), 0, 0)
    )
    return pl.pallas_call(
        tiles_kernel,
        grid_spec=pltpu.PrefetchScalarGridSpec(
            num_scalar_prefetch=2,
            grid=(steps,),
            in_specs=[taken(u) for u in range(TRIG_CHUNK)] * 2,
            out_specs=[out, out],
        ),
        out_shape=[jax.ShapeDtypeStruct((SLOTS, TILE, 2 * TILE), jnp.bfloat16)] * 2,
        compiler_params=pltpu.CompilerParams(vmem_limit_bytes=24 * MIB),
        cost_estimate=pl.CostEstimate(flops=0, bytes_accessed=60 * MIB, transcendentals=0),
        name="complex_tiles",
    )(order, count, *([weights] * TRIG_CHUNK), *([angles] * TRIG_CHUNK))


def product_kernel(sign, sizes, takes, puts, count, tiles_ref, *refs):
    x_refs = refs[: len(sizes)]
    out_ref, x_mat, acc = refs[len(sizes) :]
    step = pl.program_id(0)

    @pl.when(step == 0)
    def _():
        acc[...] = jnp.zeros_like(acc)
        low = lanes((TILE, TILE)) < 2 * WIDTH
        base = 0
        for x_ref, size in zip(x_refs, sizes):
            for p in range(size):
                value = x_ref[p, :TILE].astype(jnp.float32)
                high = value.astype(jnp.bfloat16).astype(jnp.float32)
                rest = value - high
                for k in range(2):
                    if k == 0:
                        top = jnp.where(low, high, pltpu.roll(rest, 2 * WIDTH, 1))
                    else:
                        top = jnp.where(low, pltpu.roll(high, 2 * WIDTH, 1), rest)
                    x_mat[base + 2 * p + k, :TILE] = top.astype(jnp.bfloat16)
                    x_mat[base + 2 * p + k, TILE:] = (sign * pair_swap(top)).astype(jnp.bfloat16)
            base += 2 * size

    @pl.when(step * CHUNK < count[0])
    def _():
        for u in range(CHUNK):
            slot = step * CHUNK + u
            acc[puts[slot]] += jnp.dot(
                tiles_ref[u], x_mat[takes[slot]], preferred_element_type=jnp.float32
            )

    @pl.when(step == SLOTS // CHUNK - 1)
    def _():
        low = lanes((TILE, TILE)) < 2 * WIDTH
        for p in range(out_ref.shape[0]):
            first, second = acc[2 * p], acc[2 * p + 1]
            out_ref[p] = jnp.where(
                low,
                first + pltpu.roll(first, 2 * WIDTH, 1),
                second + pltpu.roll(second, 2 * WIDTH, 1),
            )


def products(sign, takes, puts, count, tiles, sources, out_pieces, name):
    sizes = tuple(s.shape[0] for s in sources)

    def whole(s):
        return pl.BlockSpec(s.shape, lambda c, *_: (0, 0, 0))

    def chunk(c, takes, puts, count):
        return (jnp.minimum(c, pl.cdiv(count[0], CHUNK) - 1), 0, 0)

    return pl.pallas_call(
        functools.partial(product_kernel, sign, sizes),
        grid_spec=pltpu.PrefetchScalarGridSpec(
            num_scalar_prefetch=3,
            grid=(SLOTS // CHUNK,),
            in_specs=[pl.BlockSpec((CHUNK, TILE, 2 * TILE), chunk)] + [whole(s) for s in sources],
            out_specs=pl.BlockSpec((out_pieces, TILE, TILE), lambda c, *_: (0, 0, 0)),
            scratch_shapes=[
                pltpu.VMEM((2 * sum(sizes), 2 * TILE, TILE), jnp.bfloat16),
                pltpu.VMEM((2 * out_pieces, TILE, TILE), jnp.float32),
            ],
        ),
        out_shape=jax.ShapeDtypeStruct((out_pieces, TILE, TILE), jnp.float32),
        compiler_params=pltpu.CompilerParams(vmem_limit_bytes=24 * MIB),
        cost_estimate=pl.CostEstimate(flops=0, bytes_accessed=36 * MIB, transcendentals=0),
        name=name,
    )(takes, puts, count, tiles, *sources)


def gather_kernel(turned, n_parts, *refs):
    wide_ref, part_refs = refs[0], refs[1 : 1 + n_parts]
    scale_ref = refs[1 + n_parts]
    rest = refs[2 + n_parts :]
    total = wide_ref[0]
    for p in range(1, wide_ref.shape[0]):
        total = total + wide_ref[p]
    for ref in part_refs:
        total = total + ref[0]
    image = total * scale_ref[...]
    if turned:
        image = nt_dot(image, rest[0][...])
        rest = rest[1:]
    image_ref, gram_ref = rest
    image_ref[...] = image
    gram = lax.dot_general(image.T, image.T, (((1,), (1,)), ((), ())), precision=HIGHEST, preferred_element_type=jnp.float32)
    pairs = gram[: 2 * WIDTH] + pltpu.roll(gram[2 * WIDTH :], 2 * WIDTH, 1)
    upper, lower = pairs[:WIDTH], pairs[WIDTH:]
    even = lanes(upper.shape) < WIDTH
    other = jnp.where(even, pltpu.roll(lower, TILE - WIDTH, 1), -pltpu.roll(lower, WIDTH, 1))
    both = upper + other
    low = lanes((WIDTH // 2, TILE)) < 2 * WIDTH
    gram_ref[...] = jnp.where(
        low, both[: WIDTH // 2], pltpu.roll(both[WIDTH // 2 :], 2 * WIDTH, 1)
    )


def nt_dot(left, right):
    return lax.dot_general(
        left, right, (((1,), (1,)), ((), ())), precision=HIGHEST, preferred_element_type=jnp.float32
    )


def new_image(wide, parts, scale, turn):
    operands = [wide, *parts, scale] + ([] if turn is None else [turn])
    return pl.pallas_call(
        functools.partial(gather_kernel, turn is not None, len(parts)),
        out_shape=[
            jax.ShapeDtypeStruct((TILE, TILE), jnp.float32),
            jax.ShapeDtypeStruct((WIDTH // 2, TILE), jnp.float32),
        ],
        compiler_params=pltpu.CompilerParams(vmem_limit_bytes=16 * MIB),
        cost_estimate=pl.CostEstimate(flops=0, bytes_accessed=6 * MIB, transcendentals=0),
        name="new_image",
    )(*operands)


def turn_kernel(gram_ref, turn_ref):
    packed = gram_ref[...] * (1.0 / IMAGES)
    lane = lanes((WIDTH, TILE))
    place = lax.broadcasted_iota(jnp.int32, (WIDTH, TILE), 0)
    value = jnp.concatenate([packed, pltpu.roll(packed, 2 * WIDTH, 1)], axis=0)
    value = jnp.where(lane < 2 * WIDTH, value, 0.0)
    diagonal = lane == place
    trace = jnp.sum(jnp.where(diagonal, value, 0.0))
    ridge = 0.01 * trace / WIDTH + 1e-6
    value = value + jnp.where(diagonal, ridge, 0.0)
    value = value + jnp.where(lane == place + 2 * WIDTH, 1.0, 0.0)
    for column in range(WIDTH):
        row = value[column : column + 1]
        inverse = 1.0 / row[:, column : column + 1]
        below = lax.broadcasted_iota(jnp.int32, (WIDTH, 1), 0) > column
        real = jnp.where(below, value[:, column : column + 1] * inverse, 0.0)
        imag = jnp.where(below, value[:, WIDTH + column : WIDTH + column + 1] * inverse, 0.0)
        value = value - (real * row + imag * pair_swap(row))
    pivot = jnp.sum(jnp.where(diagonal, value, 0.0), axis=1, keepdims=True)
    value = value * lax.rsqrt(pivot)
    high = lane >= 2 * WIDTH
    second = jnp.where(high, value, 0.0)
    first = pltpu.roll(second, 2 * WIDTH, 1)
    turn_ref[0:WIDTH] = first
    turn_ref[WIDTH : 2 * WIDTH] = pair_swap(first)
    turn_ref[2 * WIDTH : 3 * WIDTH] = second
    turn_ref[3 * WIDTH :] = pair_swap(second)


def turn_of(gram):
    return pl.pallas_call(
        turn_kernel,
        out_shape=jax.ShapeDtypeStruct((TILE, TILE), jnp.float32),
        cost_estimate=pl.CostEstimate(flops=0, bytes_accessed=12 * MIB, transcendentals=0),
        name="turn",
    )(gram)


def basis_kernel(image_ref, turn_ref, out_ref):
    out_ref[...] = nt_dot(image_ref[...], turn_ref[...]).T


def last_basis(image, turn):
    return pl.pallas_call(
        basis_kernel,
        out_shape=jax.ShapeDtypeStruct((TILE, TILE), jnp.float32),
        name="basis",
    )(image, turn)


def along_x(value, step):
    return lax.ppermute(value, "row", [(i, (i + 2 * step) % 8) for i in range(8)])


def other_core(value):
    return lax.ppermute(value, "row", [(i, i ^ 1) for i in range(8)])


def along_col(value, z_step, y_step):
    return lax.ppermute(
        value,
        "col",
        [(i, (i // 4 + z_step) % 4 * 4 + (i % 4 + y_step) % 4) for i in range(16)],
    )


def to_column(value):
    return lax.all_to_all(value, "col", split_axis=0, concat_axis=0, tiled=True)


def gather_row(value):
    mine = jnp.stack([value] + [along_x(value, d) for d in (1, 2, 3)], 0)
    return mine, other_core(mine)


def reduce_row(value):
    half = value.shape[0] // 2
    mine = value[:half] + other_core(value[half:])
    return [mine[0:1]] + [along_x(mine[d : d + 1], d) for d in (1, 2, 3)]


def sum_row(value):
    value = value + other_core(value)
    return value + along_x(value, 1) + along_x(value, 2) + along_x(value, 3)


def sum_all(value):
    value = sum_row(value)
    value = value + along_col(value, 1, 0) + along_col(value, 2, 0) + along_col(value, 3, 0)
    return value + along_col(value, 0, 1) + along_col(value, 0, 2) + along_col(value, 0, 3)


def shards(tile_weight, tile_angle, tile_list, tile_count, init_basis):
    place = lax.axis_index("row")
    x_place, core = place // 2, place % 2
    weights = tile_weight.reshape(SLOTS, TILE, TILE)
    angles = tile_angle.reshape(SLOTS, TILE, TILE)
    listing = tile_list.reshape(SLOTS, 2)
    row_of = listing[:, 0] % ROW_BLOCKS
    col_global = listing[:, 1]
    piece = col_global // ROW_BLOCKS
    core_away = (piece % 2) ^ core
    col_from = (core_away * 4 + (x_place - piece // 2) % 4) * 2 + col_global % 2
    col_to = (core_away * 4 + (piece // 2 - x_place) % 4) * 2 + col_global % 2
    live = (jnp.arange(2)[None, :] < tile_count.reshape(SLOTS // 2, 1)).reshape(SLOTS).astype(jnp.int32)
    slots = jnp.arange(SLOTS, dtype=jnp.int32)
    earlier = slots[None, :] < slots[:, None]
    count = jnp.sum(live)
    live_before = jnp.sum(jnp.where(earlier, live[None, :], 0), axis=1)
    at = jnp.where(live > 0, live_before, count + slots - live_before)
    code = slots + SLOTS * (col_from + COL_BLOCKS * (col_to + COL_BLOCKS * row_of))
    code = jnp.sum(jnp.where(at[None, :] == slots[:, None], code[None, :], 0), axis=1)
    order = code % SLOTS
    takes_col = code // SLOTS % COL_BLOCKS
    puts_col = code // (SLOTS * COL_BLOCKS) % COL_BLOCKS
    rows = code // (SLOTS * COL_BLOCKS * COL_BLOCKS)
    count = count.reshape(1)

    row_part, col_part = degrees(row_of, col_to, live, weights)
    row_part = to_column(row_part)
    col_parts = reduce_row(col_part)
    degree = jnp.sum(row_part, axis=0) + sum(c[0] for c in col_parts)
    scale = lax.rsqrt(degree[:2])
    scale = jnp.broadcast_to(scale.T[:, :, None], (TILE, 2, 2 * WIDTH)).reshape(TILE, TILE)
    plain, turned = complex_tiles(order, count, weights, angles)

    basis = jnp.transpose(init_basis.reshape(2, WIDTH, 2, TILE), (3, 2, 0, 1)).reshape(TILE, TILE)
    sent = (basis * scale).astype(jnp.bfloat16)
    turn, gram = None, None
    for rounds in range(ITERS):
        near, far = gather_row(sent)
        body = sent if gram is None else jnp.concatenate([sent, gram], 0)
        column = to_column(jnp.broadcast_to(body[None], (16,) + body.shape))
        forward = products(1.0, takes_col, rows, count, plain, [near, far], 16, "forward")
        mirror = products(-1.0, rows, puts_col, count, turned, [column], 8, "mirror")
        wide = to_column(forward)
        parts = reduce_row(mirror)
        if gram is not None:
            turn = turn_of(sum_row(jnp.sum(column[:, TILE:], axis=0)))
        image, gram = new_image(wide, parts, scale, turn)
        sent = image * scale
    basis = last_basis(image, turn_of(sum_all(gram)))
    return jnp.transpose(basis.reshape(2, 2, WIDTH, TILE), (1, 2, 0, 3)).reshape(2, WIDTH, 2 * TILE)


def solution(mesh):
    placed = (
        P(("row", "col"), None, None, None, None),
        P(("row", "col"), None, None, None, None),
        P(("row", "col"), None, None, None),
        P(("row", "col"), None),
        P(None, None, ("row", "col")),
    )
    return jax.shard_map(
        shards, mesh=mesh, in_specs=placed, out_specs=P(None, None, ("row", "col")), check_vma=False
    )
```

```python
import functools

import jax
import jax.numpy as jnp
from jax import lax
from jax.experimental import pallas as pl
from jax.experimental.pallas import tpu as pltpu
from jax.sharding import PartitionSpec as P

ITERS = 3
IMAGES = 32768
TILE = 128
WIDTH = 32
SLOTS = 256
ROW_BLOCKS = 32
COL_BLOCKS = 16
CHUNK = 16
TRIG_CHUNK = 8
RING = 4
HALF_SIN = (0.5, -0.020833322778344154, 0.00026040783268399537, -1.5475804957532091e-06, 5.088141019626846e-09)
HALF_COS = (0.9999999403953552, -0.1249997615814209, 0.0026039734948426485, -2.164632678613998e-05, 9.044046578310372e-08)
HIGHEST = lax.Precision.HIGHEST
MIB = 1 << 20


def horner(u, coefs):
    value = coefs[-1]
    for coef in coefs[-2::-1]:
        value = value * u + coef
    return value


def lanes(shape):
    return lax.broadcasted_iota(jnp.int32, shape, 1)


def pair_swap(x):
    even = (lanes(x.shape) // WIDTH) % 2 == 0
    return jnp.where(even, -pltpu.roll(x, TILE - WIDTH, 1), pltpu.roll(x, WIDTH, 1))


VECTOR = pl.BlockSpec(memory_space=pltpu.VMEM)
SCALAR = pl.BlockSpec(memory_space=pltpu.SMEM)


FAR = pl.BlockSpec(memory_space=pl.ANY)


def fetch(source, target, sems, c):
    part = pl.ds(c * CHUNK, CHUNK)
    return pltpu.make_async_copy(source.at[part], target.at[part], sems.at[c])


def start_fetches(source, target, sems, chunks):
    def start(c, carry):
        fetch(source, target, sems, c).start()
        return carry

    lax.fori_loop(0, chunks, start, 0)


def degree_kernel(rows_of, cols_of, live, far_ref, row_ref, col_ref, row_acc, col_acc, w_ref, sems):
    start_fetches(far_ref, w_ref, sems, SLOTS // CHUNK)
    row_acc[...] = jnp.zeros_like(row_acc)
    col_acc[...] = jnp.zeros_like(col_acc)

    def step(c, carry):
        fetch(far_ref, w_ref, sems, c).wait()
        for u in range(CHUNK):
            slot = c * CHUNK + u

            @pl.when(live[slot] > 0)
            def _():
                w = w_ref[slot].astype(jnp.float32)
                row_acc[rows_of[slot]] += w
                col_acc[cols_of[slot]] += jnp.sum(w.reshape(TILE // 8, 8, TILE), axis=0)

        return carry

    lax.fori_loop(0, SLOTS // CHUNK, step, 0)
    for p in range(ROW_BLOCKS // 2):
        sums = [jnp.sum(row_acc[2 * p + k].T, axis=0, keepdims=True) for k in range(2)]
        row_ref[p] = 0.5 * jnp.concatenate(sums * 4, axis=0)
    for p in range(COL_BLOCKS // 2):
        sums = [jnp.sum(col_acc[2 * p + k], axis=0, keepdims=True) for k in range(2)]
        col_ref[p] = 0.5 * jnp.concatenate(sums * 4, axis=0)


def degrees(rows_of, cols_of, live, weights):
    return pl.pallas_call(
        degree_kernel,
        in_specs=[SCALAR, SCALAR, SCALAR, FAR],
        out_specs=[VECTOR, VECTOR],
        scratch_shapes=[
            pltpu.VMEM((ROW_BLOCKS, TILE, TILE), jnp.float32),
            pltpu.VMEM((COL_BLOCKS, 8, TILE), jnp.float32),
            pltpu.VMEM((SLOTS, TILE, TILE), jnp.bfloat16),
            pltpu.SemaphoreType.DMA((SLOTS // CHUNK,)),
        ],
        out_shape=[
            jax.ShapeDtypeStruct((ROW_BLOCKS // 2, 8, TILE), jnp.float32),
            jax.ShapeDtypeStruct((COL_BLOCKS // 2, 8, TILE), jnp.float32),
        ],
        compiler_params=pltpu.CompilerParams(vmem_limit_bytes=58 * MIB),
        cost_estimate=pl.CostEstimate(flops=0, bytes_accessed=18 * MIB, transcendentals=0),
        name="degrees",
    )(rows_of, cols_of, live, weights)


def tiles_kernel(
    order, count, far_w, far_a, far_plain, far_turned, done_ref, w_buf, a_buf, plain, turned, in_sems, out_sems
):
    done_ref[...] = jnp.zeros_like(done_ref)
    chunks = pl.cdiv(count[0], CHUNK) * (CHUNK // TRIG_CHUNK)

    def incoming(c):
        ring = c % RING
        for u in range(TRIG_CHUNK):
            source = order[c * TRIG_CHUNK + u]
            yield pltpu.make_async_copy(far_w.at[source], w_buf.at[ring, u], in_sems.at[ring, 0, u])
            yield pltpu.make_async_copy(far_a.at[source], a_buf.at[ring, u], in_sems.at[ring, 1, u])

    def outgoing(c):
        part = pl.ds(c * TRIG_CHUNK, TRIG_CHUNK)
        yield pltpu.make_async_copy(plain.at[c % 2], far_plain.at[part], out_sems.at[c % 2, 0])
        yield pltpu.make_async_copy(turned.at[c % 2], far_turned.at[part], out_sems.at[c % 2, 1])

    def begin(c):
        @pl.when(c < chunks)
        def _():
            for copy in incoming(c):
                copy.start()

    for c in range(RING - 1):
        begin(jnp.int32(c))

    def step(c, carry):
        begin(c + RING - 1)
        for copy in incoming(c):
            copy.wait()

        @pl.when(c >= 2)
        def _():
            for copy in outgoing(c - 2):
                copy.wait()

        ring, side = c % RING, c % 2
        for u in range(TRIG_CHUNK):
            half = jnp.where(c * TRIG_CHUNK + u < count[0], 0.5, 0.0).astype(jnp.float32)
            theta = a_buf[ring, u].astype(jnp.float32)
            w = w_buf[ring, u].astype(jnp.float32) * half
            square = theta * theta
            sine = theta * horner(square, HALF_SIN)
            cosine = horner(square, HALF_COS)
            part = (w + w) * sine
            real = w - part * sine
            imag = part * cosine
            plain[side, u, :, :TILE] = real.astype(jnp.bfloat16)
            plain[side, u, :, TILE:] = imag.astype(jnp.bfloat16)
            turned[side, u, :, :TILE] = real.T.astype(jnp.bfloat16)
            turned[side, u, :, TILE:] = imag.T.astype(jnp.bfloat16)
        for copy in outgoing(c):
            copy.start()
        return carry

    lax.fori_loop(0, chunks, step, 0)
    for back in (2, 1):
        for copy in outgoing(chunks - back):
            copy.wait()


def complex_tiles(order, count, weights, angles):
    return pl.pallas_call(
        tiles_kernel,
        in_specs=[SCALAR, SCALAR, FAR, FAR],
        out_specs=[FAR, FAR, VECTOR],
        out_shape=[jax.ShapeDtypeStruct((SLOTS, TILE, 2 * TILE), jnp.bfloat16)] * 2
        + [jax.ShapeDtypeStruct((8, TILE), jnp.float32)],
        scratch_shapes=[
            pltpu.VMEM((RING, TRIG_CHUNK, TILE, TILE), jnp.bfloat16),
            pltpu.VMEM((RING, TRIG_CHUNK, TILE, TILE), jnp.bfloat16),
            pltpu.VMEM((2, TRIG_CHUNK, TILE, 2 * TILE), jnp.bfloat16),
            pltpu.VMEM((2, TRIG_CHUNK, TILE, 2 * TILE), jnp.bfloat16),
            pltpu.SemaphoreType.DMA((RING, 2, TRIG_CHUNK)),
            pltpu.SemaphoreType.DMA((2, 2)),
        ],
        compiler_params=pltpu.CompilerParams(vmem_limit_bytes=58 * MIB),
        cost_estimate=pl.CostEstimate(flops=0, bytes_accessed=50 * MIB, transcendentals=0),
        name="complex_tiles",
    )(order, count, weights, angles)


def product_kernel(sign, sizes, takes, puts, count, far_ref, *refs):
    x_refs = refs[: len(sizes)]
    out_ref, x_mat, acc, tiles_ref, sems = refs[len(sizes) :]
    chunks = pl.cdiv(count[0], CHUNK)
    start_fetches(far_ref, tiles_ref, sems, chunks)
    low = lanes((TILE, TILE)) < 2 * WIDTH
    acc[...] = jnp.zeros_like(acc)
    base = 0
    for x_ref, size in zip(x_refs, sizes):
        for p in range(size):
            value = x_ref[p, :TILE].astype(jnp.float32)
            high = value.astype(jnp.bfloat16).astype(jnp.float32)
            rest = value - high
            for k in range(2):
                if k == 0:
                    top = jnp.where(low, high, pltpu.roll(rest, 2 * WIDTH, 1))
                else:
                    top = jnp.where(low, pltpu.roll(high, 2 * WIDTH, 1), rest)
                x_mat[base + 2 * p + k, :TILE] = top.astype(jnp.bfloat16)
                x_mat[base + 2 * p + k, TILE:] = (sign * pair_swap(top)).astype(jnp.bfloat16)
        base += 2 * size

    def step(c, carry):
        fetch(far_ref, tiles_ref, sems, c).wait()
        for u in range(CHUNK):
            slot = c * CHUNK + u
            acc[puts[slot]] += jnp.dot(
                tiles_ref[slot], x_mat[takes[slot]], preferred_element_type=jnp.float32
            )
        return carry

    lax.fori_loop(0, chunks, step, 0)
    if out_ref.shape[1] > TILE:
        gram = x_refs[0][0, TILE:]
        for p in range(1, sizes[0]):
            gram = gram + x_refs[0][p, TILE:]
    for p in range(out_ref.shape[0]):
        if out_ref.shape[1] > TILE:
            out_ref[p, TILE:] = gram
        first, second = acc[2 * p], acc[2 * p + 1]
        out_ref[p, :TILE] = jnp.where(
            low,
            first + pltpu.roll(first, 2 * WIDTH, 1),
            second + pltpu.roll(second, 2 * WIDTH, 1),
        )


def products(sign, takes, puts, count, tiles, sources, out_shape, name):
    sizes = tuple(s.shape[0] for s in sources)
    return pl.pallas_call(
        functools.partial(product_kernel, sign, sizes),
        in_specs=[SCALAR, SCALAR, SCALAR, FAR] + [VECTOR] * len(sources),
        out_specs=VECTOR,
        scratch_shapes=[
            pltpu.VMEM((2 * sum(sizes), 2 * TILE, TILE), jnp.bfloat16),
            pltpu.VMEM((2 * out_shape[0], TILE, TILE), jnp.float32),
            pltpu.VMEM((SLOTS, TILE, 2 * TILE), jnp.bfloat16),
            pltpu.SemaphoreType.DMA((SLOTS // CHUNK,)),
        ],
        out_shape=jax.ShapeDtypeStruct(out_shape, jnp.float32),
        compiler_params=pltpu.CompilerParams(vmem_limit_bytes=52 * MIB),
        cost_estimate=pl.CostEstimate(flops=0, bytes_accessed=30 * MIB, transcendentals=0),
        name=name,
    )(takes, puts, count, tiles, *sources)


def gather_kernel(turned, final, n_parts, *refs):
    wide_ref, part_refs = refs[0], refs[1 : 1 + n_parts]
    scale_ref = refs[1 + n_parts]
    rest = refs[2 + n_parts :]
    total = wide_ref[0]
    for p in range(1, wide_ref.shape[0]):
        total = total + wide_ref[p]
    for ref in part_refs:
        total = total + ref[0, :TILE]
    scale = scale_ref[...]
    image = total * scale
    if turned:
        image = nt_dot(image, rest[0][...])
        rest = rest[1:]
    across = image.T
    gram = nt_dot(across, across)
    pairs = gram[: 2 * WIDTH] + pltpu.roll(gram[2 * WIDTH :], 2 * WIDTH, 1)
    upper, lower = pairs[:WIDTH], pairs[WIDTH:]
    lane = lanes(upper.shape)
    other = jnp.where(lane < WIDTH, pltpu.roll(lower, TILE - WIDTH, 1), -pltpu.roll(lower, WIDTH, 1))
    both = upper + other
    if final:
        image_ref, gram_ref = rest
        image_ref[...] = image
        row = lax.broadcasted_iota(jnp.int32, upper.shape, 0)
        packed = jnp.where(lane >= row, both, pltpu.roll(both, TILE - WIDTH, 1))
        out = packed[:8]
        group = lanes((8, TILE)) // WIDTH
        for g in range(1, 4):
            out = jnp.where(group == g, pltpu.roll(packed[8 * g : 8 * g + 8], WIDTH * g, 1), out)
        gram_ref[0] = out
    else:
        sent_ref, body_ref = rest
        value = image * scale
        sent_ref[...] = value
        body_ref[:TILE] = value
        low = lanes((WIDTH // 2, TILE)) < 2 * WIDTH
        body_ref[TILE:] = jnp.where(
            low, both[: WIDTH // 2], pltpu.roll(both[WIDTH // 2 :], 2 * WIDTH, 1)
        )


def nt_dot(left, right):
    return lax.dot_general(
        left, right, (((1,), (1,)), ((), ())), precision=HIGHEST, preferred_element_type=jnp.float32
    )


def new_image(wide, parts, scale, turn, final):
    operands = [wide, *parts, scale] + ([] if turn is None else [turn])
    second = (1, 8, TILE) if final else (TILE + WIDTH // 2, TILE)
    return pl.pallas_call(
        functools.partial(gather_kernel, turn is not None, final, len(parts)),
        out_shape=[
            jax.ShapeDtypeStruct((TILE, TILE), jnp.float32),
            jax.ShapeDtypeStruct(second, jnp.float32),
        ],
        compiler_params=pltpu.CompilerParams(vmem_limit_bytes=6 * MIB),
        cost_estimate=pl.CostEstimate(flops=0, bytes_accessed=6 * MIB, transcendentals=0),
        name="new_image",
    )(*operands)


def spread(x, lane):
    return jnp.broadcast_to(x[:, lane : lane + 1], (8, TILE))


def invert_factor(value, turn_ref):
    size = 4
    lane = lanes((WIDTH, TILE))
    place = lax.broadcasted_iota(jnp.int32, (WIDTH, TILE), 0)
    diagonal = lane == place
    trace = jnp.sum(jnp.where(diagonal, value, 0.0))
    ridge = 0.01 * trace / WIDTH + 1e-6
    value = value + jnp.where(diagonal, ridge, 0.0)
    value = value + jnp.where(lane == place + 2 * WIDTH, 1.0, 0.0)
    groups = [value[8 * g : 8 * g + 8] for g in range(4)]
    within = lax.broadcasted_iota(jnp.int32, (8, TILE), 0)
    for c in range(0, WIDTH, size):
        g, o = c // 8, c % 8
        rows = [jnp.broadcast_to(groups[g][o + r : o + r + 1], (8, TILE)) for r in range(size)]
        turned = [pair_swap(row) for row in rows]
        block = {
            (r, k): (spread(rows[r], c + k), spread(rows[r], WIDTH + c + k))
            for r in range(size)
            for k in range(r, size)
        }
        below = list(range(g if o + size < 8 else g + 1, 4))
        cols = {
            (h, k): (spread(groups[h], c + k), spread(groups[h], WIDTH + c + k))
            for h in below
            for k in range(size)
        }
        new = {h: groups[h] for h in below}
        for k in range(size):
            inverse = 1.0 / block[k, k][0]
            for r in range(k + 1, size):
                real, imag = block[k, r][0] * inverse, -block[k, r][1] * inverse
                rows[r], turned[r] = (
                    rows[r] - (real * rows[k] + imag * turned[k]),
                    turned[r] - (real * turned[k] - imag * rows[k]),
                )
                for j in range(r, size):
                    other = block[k, j]
                    block[r, j] = (
                        block[r, j][0] - (real * other[0] - imag * other[1]),
                        block[r, j][1] - (real * other[1] + imag * other[0]),
                    )
            for h in below:
                real, imag = cols[h, k][0] * inverse, cols[h, k][1] * inverse
                for j in range(k + 1, size):
                    other = block[k, j]
                    cols[h, j] = (
                        cols[h, j][0] - (real * other[0] - imag * other[1]),
                        cols[h, j][1] - (real * other[1] + imag * other[0]),
                    )
                step = real * rows[k] + imag * turned[k]
                new[h] = new[h] - (jnp.where(within >= o + size, step, 0.0) if h == g else step)
        kept = new.get(g, groups[g])
        for r in range(size):
            kept = jnp.where(within == o + r, rows[r], kept)
        for h in below:
            groups[h] = new[h]
        groups[g] = kept
    value = jnp.concatenate(groups, axis=0)
    pivot = jnp.sum(jnp.where(diagonal, value, 0.0), axis=1, keepdims=True)
    value = value * lax.rsqrt(pivot)
    second = jnp.where(lane >= 2 * WIDTH, value, 0.0)
    first = pltpu.roll(second, 2 * WIDTH, 1)
    turn_ref[0:WIDTH] = first
    turn_ref[WIDTH : 2 * WIDTH] = pair_swap(first)
    turn_ref[2 * WIDTH : 3 * WIDTH] = second
    turn_ref[3 * WIDTH :] = pair_swap(second)


def turn_kernel(*refs):
    part_refs, turn_ref = refs[:-1], refs[-1]
    packed = part_refs[0][0, TILE:]
    for ref in part_refs[1:]:
        packed = packed + ref[0, TILE:]
    packed = packed * (1.0 / IMAGES)
    value = jnp.concatenate([packed, pltpu.roll(packed, 2 * WIDTH, 1)], axis=0)
    invert_factor(jnp.where(lanes(value.shape) < 2 * WIDTH, value, 0.0), turn_ref)


def turn_of(parts):
    return pl.pallas_call(
        turn_kernel,
        out_shape=jax.ShapeDtypeStruct((TILE, TILE), jnp.float32),
        compiler_params=pltpu.CompilerParams(vmem_limit_bytes=6 * MIB),
        cost_estimate=pl.CostEstimate(flops=0, bytes_accessed=9 * MIB, transcendentals=0),
        name="turn",
    )(*parts)


def basis_kernel(image_ref, gram_ref, out_ref, turn_ref):
    packed = jnp.sum(gram_ref[...], axis=0) * (1.0 / IMAGES)
    value = jnp.concatenate(
        [packed] + [pltpu.roll(packed, TILE - WIDTH * g, 1) for g in range(1, 4)], axis=0
    )
    across = jnp.concatenate([value] + [jnp.zeros_like(value)] * 3, axis=0).T[:WIDTH]
    lane = lanes(value.shape)
    row = lax.broadcasted_iota(jnp.int32, value.shape, 0)
    real = jnp.where(lane >= row, value, across)
    imag = jnp.where(lane == row, 0.0, jnp.where(lane < row, value, -across))
    value = jnp.where(lane < WIDTH, real, 0.0)
    value = value + jnp.where((lane >= WIDTH) & (lane < 2 * WIDTH), pltpu.roll(imag, WIDTH, 1), 0.0)
    invert_factor(value, turn_ref)
    out = nt_dot(image_ref[...], turn_ref[...]).T
    for part in range(2):
        for block in range(2):
            start = (2 * block + part) * WIDTH
            out_ref[part, :, block * TILE : (block + 1) * TILE] = out[start : start + WIDTH]


def last_basis(image, grams):
    return pl.pallas_call(
        basis_kernel,
        out_shape=jax.ShapeDtypeStruct((2, WIDTH, 2 * TILE), jnp.float32),
        scratch_shapes=[pltpu.VMEM((TILE, TILE), jnp.float32)],
        compiler_params=pltpu.CompilerParams(vmem_limit_bytes=6 * MIB),
        name="basis",
    )(image, grams)


def along_x(value, step):
    return lax.ppermute(value, "row", [(i, (i + 2 * step) % 8) for i in range(8)])


def other_core(value):
    return lax.ppermute(value, "row", [(i, i ^ 1) for i in range(8)])


def to_column(value):
    return lax.all_to_all(value, "col", split_axis=0, concat_axis=0, tiled=True)


def gather_row(value):
    mine = jnp.stack([value] + [along_x(value, d) for d in (1, 2, 3)], 0)
    return mine, other_core(mine)


def reduce_row(value):
    half = value.shape[0] // 2
    mine = value[:half] + other_core(value[half:])
    return [mine[0:1]] + [along_x(mine[d : d + 1], d) for d in (1, 2, 3)]


def shards(tile_weight, tile_angle, tile_list, tile_count, init_basis):
    place = lax.axis_index("row")
    x_place, core = place // 2, place % 2
    weights = tile_weight.reshape(SLOTS, TILE, TILE)
    angles = tile_angle.reshape(SLOTS, TILE, TILE)
    listing = tile_list.reshape(SLOTS, 2)
    row_of = listing[:, 0] % ROW_BLOCKS
    col_global = listing[:, 1]
    piece = col_global // ROW_BLOCKS
    core_away = (piece % 2) ^ core
    col_from = (core_away * 4 + (x_place - piece // 2) % 4) * 2 + col_global % 2
    col_to = (core_away * 4 + (piece // 2 - x_place) % 4) * 2 + col_global % 2
    live = (jnp.arange(2)[None, :] < tile_count.reshape(SLOTS // 2, 1)).reshape(SLOTS).astype(jnp.int32)
    slots = jnp.arange(SLOTS, dtype=jnp.int32)
    earlier = slots[None, :] < slots[:, None]
    count = jnp.sum(live)
    live_before = jnp.sum(jnp.where(earlier, live[None, :], 0), axis=1)
    at = jnp.where(live > 0, live_before, count + slots - live_before)
    code = slots + SLOTS * (col_from + COL_BLOCKS * (col_to + COL_BLOCKS * row_of))
    code = jnp.sum(jnp.where(at[None, :] == slots[:, None], code[None, :], 0), axis=1)
    order = code % SLOTS
    takes_col = code // SLOTS % COL_BLOCKS
    puts_col = code // (SLOTS * COL_BLOCKS) % COL_BLOCKS
    rows = code // (SLOTS * COL_BLOCKS * COL_BLOCKS)
    count = count.reshape(1)

    row_part, col_part = degrees(row_of, col_to, live, weights)
    row_part = to_column(row_part)
    col_parts = reduce_row(col_part)
    degree = jnp.sum(row_part, axis=0) + sum(c[0] for c in col_parts)
    plain, turned, done = complex_tiles(order, count, weights, angles)
    degree = degree + done
    scale = lax.rsqrt(degree[:2])
    scale = jnp.broadcast_to(scale.T[:, :, None], (TILE, 2, 2 * WIDTH)).reshape(TILE, TILE)

    basis = jnp.transpose(init_basis.reshape(2, WIDTH, 2, TILE), (3, 2, 0, 1)).reshape(TILE, TILE)
    sent = (basis * scale).astype(jnp.bfloat16)
    body, turn = sent, None
    for rounds in range(ITERS):
        near, far = gather_row(sent)
        column = to_column(jnp.broadcast_to(body[None], (16,) + body.shape))
        forward = products(1.0, takes_col, rows, count, plain, [near, far], (16, TILE, TILE), "forward")
        mirror = products(
            -1.0, rows, puts_col, count, turned, [column], (8, body.shape[0], TILE), "mirror"
        )
        wide = to_column(forward)
        parts = reduce_row(mirror)
        if rounds > 0:
            turn = turn_of(parts)
        sent, body = new_image(wide, parts, scale, turn, rounds == ITERS - 1)
    grams = jnp.broadcast_to(body, (128, 8, TILE))
    grams = lax.all_to_all(grams, ("row", "col"), split_axis=0, concat_axis=0, tiled=True)
    return last_basis(sent, grams)


def solution(mesh):
    placed = (
        P(("row", "col"), None, None, None, None),
        P(("row", "col"), None, None, None, None),
        P(("row", "col"), None, None, None),
        P(("row", "col"), None),
        P(None, None, ("row", "col")),
    )
    return jax.shard_map(
        shards, mesh=mesh, in_specs=placed, out_specs=P(None, None, ("row", "col")), check_vma=False
    )
```

```python
import functools

import jax
import jax.numpy as jnp
from jax import lax
from jax.experimental import pallas as pl
from jax.experimental.pallas import tpu as pltpu
from jax.sharding import PartitionSpec as P

ITERS = 3
IMAGES = 32768
TILE = 128
WIDTH = 32
SLOTS = 256
ROW_BLOCKS = 32
COL_BLOCKS = 16
CHUNK = 16
TRIG_CHUNK = 8
HALF_SIN = (0.5, -0.020833322778344154, 0.00026040783268399537, -1.5475804957532091e-06, 5.088141019626846e-09)
HALF_COS = (0.9999999403953552, -0.1249997615814209, 0.0026039734948426485, -2.164632678613998e-05, 9.044046578310372e-08)
HIGHEST = lax.Precision.HIGHEST
MIB = 1 << 20


def horner(u, coefs):
    value = coefs[-1]
    for coef in coefs[-2::-1]:
        value = value * u + coef
    return value


def lanes(shape):
    return lax.broadcasted_iota(jnp.int32, shape, 1)


def pair_swap(x):
    even = (lanes(x.shape) // WIDTH) % 2 == 0
    return jnp.where(even, -pltpu.roll(x, TILE - WIDTH, 1), pltpu.roll(x, WIDTH, 1))


VECTOR = pl.BlockSpec(memory_space=pltpu.VMEM)
SCALAR = pl.BlockSpec(memory_space=pltpu.SMEM)


FAR = pl.BlockSpec(memory_space=pl.ANY)


def fetch(source, target, sems, c):
    part = pl.ds(c * CHUNK, CHUNK)
    return pltpu.make_async_copy(source.at[part], target.at[part], sems.at[c])


def start_fetches(source, target, sems, chunks):
    def start(c, carry):
        fetch(source, target, sems, c).start()
        return carry

    lax.fori_loop(0, chunks, start, 0)


def tiles_kernel(
    order, rows, cols, count, far_w, far_a, far_plain, far_turned, row_ref, col_ref,
    w_ref, a_ref, plain, turned, row_acc, col_acc, w_sems, a_sems, out_sems,
):
    def start(c, carry):
        fetch(far_w, w_ref, w_sems, c).start()
        fetch(far_a, a_ref, a_sems, c).start()
        return carry

    lax.fori_loop(0, SLOTS // CHUNK, start, 0)
    row_acc[...] = jnp.zeros_like(row_acc)
    col_acc[...] = jnp.zeros_like(col_acc)
    chunks = pl.cdiv(count[0], CHUNK) * (CHUNK // TRIG_CHUNK)

    def outgoing(c):
        part = pl.ds(c * TRIG_CHUNK, TRIG_CHUNK)
        yield pltpu.make_async_copy(plain.at[c % 2], far_plain.at[part], out_sems.at[c % 2, 0])
        yield pltpu.make_async_copy(turned.at[c % 2], far_turned.at[part], out_sems.at[c % 2, 1])

    def arrive(c, carry):
        fetch(far_w, w_ref, w_sems, c).wait()
        fetch(far_a, a_ref, a_sems, c).wait()
        return carry

    def step(c, here):
        reach = order[c * TRIG_CHUNK + TRIG_CHUNK - 1] // CHUNK + 1
        need = jnp.where(c >= chunks - CHUNK // TRIG_CHUNK, SLOTS // CHUNK, reach)
        lax.fori_loop(here, need, arrive, 0)

        @pl.when(c >= 2)
        def _():
            for copy in outgoing(c - 2):
                copy.wait()

        side = c % 2
        for u in range(TRIG_CHUNK):
            slot = c * TRIG_CHUNK + u
            source = order[slot]
            theta = a_ref[source].astype(jnp.float32)
            w = w_ref[source].astype(jnp.float32)
            square = theta * theta
            sine = theta * horner(square, HALF_SIN)
            cosine = horner(square, HALF_COS)
            part = w * sine
            real = (0.5 * w - part * sine).astype(jnp.bfloat16)
            imag = (part * cosine).astype(jnp.bfloat16)
            plain[side, u, :, :TILE] = real
            plain[side, u, :, TILE:] = imag
            turned[side, u, :, :TILE] = real.T
            turned[side, u, :, TILE:] = imag.T
            row_acc[rows[slot]] += w
            col_acc[cols[slot]] += jnp.sum(w.reshape(TILE // 8, 8, TILE), axis=0)
        for copy in outgoing(c):
            copy.start()
        return need

    lax.fori_loop(0, chunks, step, 0)
    for p in range(ROW_BLOCKS // 2):
        sums = [jnp.sum(row_acc[2 * p + k].T, axis=0, keepdims=True) for k in range(2)]
        row_ref[p] = 0.5 * jnp.concatenate(sums * 4, axis=0)
    for p in range(COL_BLOCKS // 2):
        sums = [jnp.sum(col_acc[2 * p + k], axis=0, keepdims=True) for k in range(2)]
        col_ref[p] = 0.5 * jnp.concatenate(sums * 4, axis=0)
    for back in (2, 1):
        for copy in outgoing(chunks - back):
            copy.wait()


def complex_tiles(order, rows, cols, count, weights, angles):
    return pl.pallas_call(
        tiles_kernel,
        in_specs=[SCALAR] * 4 + [FAR, FAR],
        out_specs=[FAR, FAR, VECTOR, VECTOR],
        out_shape=[jax.ShapeDtypeStruct((SLOTS, TILE, 2 * TILE), jnp.bfloat16)] * 2
        + [
            jax.ShapeDtypeStruct((ROW_BLOCKS // 2, 8, TILE), jnp.float32),
            jax.ShapeDtypeStruct((COL_BLOCKS // 2, 8, TILE), jnp.float32),
        ],
        scratch_shapes=[
            pltpu.VMEM((SLOTS, TILE, TILE), jnp.bfloat16),
            pltpu.VMEM((SLOTS, TILE, TILE), jnp.bfloat16),
            pltpu.VMEM((2, TRIG_CHUNK, TILE, 2 * TILE), jnp.bfloat16),
            pltpu.VMEM((2, TRIG_CHUNK, TILE, 2 * TILE), jnp.bfloat16),
            pltpu.VMEM((ROW_BLOCKS + 1, TILE, TILE), jnp.float32),
            pltpu.VMEM((COL_BLOCKS + 1, 8, TILE), jnp.float32),
            pltpu.SemaphoreType.DMA((SLOTS // CHUNK,)),
            pltpu.SemaphoreType.DMA((SLOTS // CHUNK,)),
            pltpu.SemaphoreType.DMA((2, 2)),
        ],
        compiler_params=pltpu.CompilerParams(vmem_limit_bytes=58 * MIB),
        cost_estimate=pl.CostEstimate(flops=0, bytes_accessed=50 * MIB, transcendentals=0),
        name="complex_tiles",
    )(order, rows, cols, count, weights, angles)


def product_kernel(sign, sizes, apart, takes, puts, count, far_ref, *refs):
    x_refs = refs[: len(sizes)]
    out_ref, x_mat, acc, tiles_ref, sems = refs[len(sizes) :][:5]
    chunks = pl.cdiv(count[0], CHUNK)
    start_fetches(far_ref, tiles_ref, sems, chunks)
    low = lanes((TILE, TILE)) < 2 * WIDTH
    acc[...] = jnp.zeros_like(acc)
    x_mat[2 * sum(sizes)] = jnp.zeros_like(x_mat[0])
    base = 0
    for x_ref, size in zip(x_refs, sizes):
        for p in range(size):
            value = x_ref[p, :TILE].astype(jnp.float32)
            high = value.astype(jnp.bfloat16).astype(jnp.float32)
            rest = value - high
            for k in range(2):
                if k == 0:
                    top = jnp.where(low, high, pltpu.roll(rest, 2 * WIDTH, 1))
                else:
                    top = jnp.where(low, pltpu.roll(high, 2 * WIDTH, 1), rest)
                x_mat[base + 2 * p + k, :TILE] = top.astype(jnp.bfloat16)
                x_mat[base + 2 * p + k, TILE:] = (sign * pair_swap(top)).astype(jnp.bfloat16)
        base += 2 * size

    def step(c, carry):
        fetch(far_ref, tiles_ref, sems, c).wait()
        for u in range(CHUNK):
            slot = c * CHUNK + u
            acc[puts[slot]] += jnp.dot(
                tiles_ref[slot], x_mat[takes[slot]], preferred_element_type=jnp.float32
            )
        return carry

    lax.fori_loop(0, chunks, step, 0)
    near, out_sems = refs[len(sizes) :][5:] if apart else (out_ref, None)
    if out_ref.shape[1] > TILE:
        gram = sum(x_ref[p, TILE:] for x_ref, size in zip(x_refs, sizes) for p in range(size))
    copies = []
    for p in range(out_ref.shape[0]):
        if out_ref.shape[1] > TILE:
            near[p, TILE:] = gram
        first, second = acc[2 * p], acc[2 * p + 1]
        near[p, :TILE] = jnp.where(
            low,
            first + pltpu.roll(first, 2 * WIDTH, 1),
            second + pltpu.roll(second, 2 * WIDTH, 1),
        )
        if apart:
            copies.append(pltpu.make_async_copy(near.at[p], out_ref.at[p], out_sems.at[p]))
            copies[-1].start()
    for copy in copies:
        copy.wait()


def products(sign, takes, puts, count, tiles, sources, out_shape, apart, name):
    sizes = tuple(s.shape[0] for s in sources)
    scratch = [
        pltpu.VMEM((2 * sum(sizes) + 1, 2 * TILE, TILE), jnp.bfloat16),
        pltpu.VMEM((2 * out_shape[0] + 1, TILE, TILE), jnp.float32),
        pltpu.VMEM((SLOTS, TILE, 2 * TILE), jnp.bfloat16),
        pltpu.SemaphoreType.DMA((SLOTS // CHUNK,)),
    ]
    if apart:
        scratch += [pltpu.VMEM(out_shape, jnp.float32), pltpu.SemaphoreType.DMA((out_shape[0],))]
    return pl.pallas_call(
        functools.partial(product_kernel, sign, sizes, apart),
        in_specs=[SCALAR, SCALAR, SCALAR, FAR] + [VECTOR] * len(sources),
        out_specs=FAR if apart else VECTOR,
        scratch_shapes=scratch,
        out_shape=jax.ShapeDtypeStruct(out_shape, jnp.float32),
        compiler_params=pltpu.CompilerParams(vmem_limit_bytes=52 * MIB),
        cost_estimate=pl.CostEstimate(flops=0, bytes_accessed=30 * MIB, transcendentals=0),
        name=name,
    )(takes, puts, count, tiles, *sources)


def gather_kernel(turned, final, n_parts, *refs):
    wide_ref, part_refs = refs[0], refs[1 : 1 + n_parts]
    scale_ref = refs[1 + n_parts]
    rest = refs[2 + n_parts :]
    total = wide_ref[0, :TILE]
    for p in range(1, wide_ref.shape[0]):
        total = total + wide_ref[p, :TILE]
    for ref in part_refs:
        total = total + ref[0]
    scale = scale_ref[...]
    image = total * scale
    if turned:
        image = nt_dot(image, rest[0][...])
        rest = rest[1:]
    across = image.T
    gram = nt_dot(across, across)
    pairs = gram[: 2 * WIDTH] + pltpu.roll(gram[2 * WIDTH :], 2 * WIDTH, 1)
    upper, lower = pairs[:WIDTH], pairs[WIDTH:]
    lane = lanes(upper.shape)
    other = jnp.where(lane < WIDTH, pltpu.roll(lower, TILE - WIDTH, 1), -pltpu.roll(lower, WIDTH, 1))
    both = upper + other
    if final:
        image_ref, gram_ref = rest
        image_ref[...] = image
        row = lax.broadcasted_iota(jnp.int32, upper.shape, 0)
        packed = jnp.where(lane >= row, both, pltpu.roll(both, TILE - WIDTH, 1))
        out = packed[:8]
        group = lanes((8, TILE)) // WIDTH
        for g in range(1, 4):
            out = jnp.where(group == g, pltpu.roll(packed[8 * g : 8 * g + 8], WIDTH * g, 1), out)
        gram_ref[0] = out
    else:
        sent_ref, body_ref = rest
        value = image * scale
        sent_ref[...] = value
        body_ref[:TILE] = value
        low = lanes((WIDTH // 2, TILE)) < 2 * WIDTH
        body_ref[TILE:] = jnp.where(
            low, both[: WIDTH // 2], pltpu.roll(both[WIDTH // 2 :], 2 * WIDTH, 1)
        )


def nt_dot(left, right):
    return lax.dot_general(
        left, right, (((1,), (1,)), ((), ())), precision=HIGHEST, preferred_element_type=jnp.float32
    )


def new_image(wide, parts, scale, turn, final):
    operands = [wide, *parts, scale] + ([] if turn is None else [turn])
    second = (1, 8, TILE) if final else (TILE + WIDTH // 2, TILE)
    return pl.pallas_call(
        functools.partial(gather_kernel, turn is not None, final, len(parts)),
        out_shape=[
            jax.ShapeDtypeStruct((TILE, TILE), jnp.float32),
            jax.ShapeDtypeStruct(second, jnp.float32),
        ],
        compiler_params=pltpu.CompilerParams(vmem_limit_bytes=6 * MIB),
        cost_estimate=pl.CostEstimate(flops=0, bytes_accessed=6 * MIB, transcendentals=0),
        name="new_image",
    )(*operands)


def spread(x, lane):
    return jnp.broadcast_to(x[:, lane : lane + 1], (8, TILE))


def invert_factor(value, turn_ref):
    size = 4
    lane = lanes((WIDTH, TILE))
    place = lax.broadcasted_iota(jnp.int32, (WIDTH, TILE), 0)
    diagonal = lane == place
    trace = jnp.sum(jnp.where(diagonal, value, 0.0))
    ridge = 0.01 * trace / WIDTH + 1e-6
    value = value + jnp.where(diagonal, ridge, 0.0)
    value = value + jnp.where(lane == place + 2 * WIDTH, 1.0, 0.0)
    groups = [value[8 * g : 8 * g + 8] for g in range(4)]
    within = lax.broadcasted_iota(jnp.int32, (8, TILE), 0)
    for c in range(0, WIDTH, size):
        g, o = c // 8, c % 8
        rows = [jnp.broadcast_to(groups[g][o + r : o + r + 1], (8, TILE)) for r in range(size)]
        turned = [pair_swap(row) for row in rows]
        block = {
            (r, k): (spread(rows[r], c + k), spread(rows[r], WIDTH + c + k))
            for r in range(size)
            for k in range(r, size)
        }
        below = list(range(g if o + size < 8 else g + 1, 4))
        cols = {
            (h, k): (spread(groups[h], c + k), spread(groups[h], WIDTH + c + k))
            for h in below
            for k in range(size)
        }
        new = {h: groups[h] for h in below}
        for k in range(size):
            inverse = 1.0 / block[k, k][0]
            for r in range(k + 1, size):
                real, imag = block[k, r][0] * inverse, -block[k, r][1] * inverse
                rows[r], turned[r] = (
                    rows[r] - (real * rows[k] + imag * turned[k]),
                    turned[r] - (real * turned[k] - imag * rows[k]),
                )
                for j in range(r, size):
                    other = block[k, j]
                    block[r, j] = (
                        block[r, j][0] - (real * other[0] - imag * other[1]),
                        block[r, j][1] - (real * other[1] + imag * other[0]),
                    )
            for h in below:
                real, imag = cols[h, k][0] * inverse, cols[h, k][1] * inverse
                for j in range(k + 1, size):
                    other = block[k, j]
                    cols[h, j] = (
                        cols[h, j][0] - (real * other[0] - imag * other[1]),
                        cols[h, j][1] - (real * other[1] + imag * other[0]),
                    )
                step = real * rows[k] + imag * turned[k]
                new[h] = new[h] - (jnp.where(within >= o + size, step, 0.0) if h == g else step)
        kept = new.get(g, groups[g])
        for r in range(size):
            kept = jnp.where(within == o + r, rows[r], kept)
        for h in below:
            groups[h] = new[h]
        groups[g] = kept
    value = jnp.concatenate(groups, axis=0)
    pivot = jnp.sum(jnp.where(diagonal, value, 0.0), axis=1, keepdims=True)
    value = value * lax.rsqrt(pivot)
    second = jnp.where(lane >= 2 * WIDTH, value, 0.0)
    first = pltpu.roll(second, 2 * WIDTH, 1)
    turn_ref[0:WIDTH] = first
    turn_ref[WIDTH : 2 * WIDTH] = pair_swap(first)
    turn_ref[2 * WIDTH : 3 * WIDTH] = second
    turn_ref[3 * WIDTH :] = pair_swap(second)


def turn_kernel(wide_ref, turn_ref):
    packed = wide_ref[0, TILE:]
    for p in range(1, wide_ref.shape[0]):
        packed = packed + wide_ref[p, TILE:]
    packed = packed * (1.0 / IMAGES)
    value = jnp.concatenate([packed, pltpu.roll(packed, 2 * WIDTH, 1)], axis=0)
    invert_factor(jnp.where(lanes(value.shape) < 2 * WIDTH, value, 0.0), turn_ref)


def turn_of(wide):
    return pl.pallas_call(
        turn_kernel,
        out_shape=jax.ShapeDtypeStruct((TILE, TILE), jnp.float32),
        compiler_params=pltpu.CompilerParams(vmem_limit_bytes=6 * MIB),
        cost_estimate=pl.CostEstimate(flops=0, bytes_accessed=6 * MIB, transcendentals=0),
        name="turn",
    )(wide)


def basis_kernel(image_ref, gram_ref, out_ref, turn_ref):
    packed = jnp.sum(gram_ref[...], axis=0) * (1.0 / IMAGES)
    value = jnp.concatenate(
        [packed] + [pltpu.roll(packed, TILE - WIDTH * g, 1) for g in range(1, 4)], axis=0
    )
    across = jnp.concatenate([value] + [jnp.zeros_like(value)] * 3, axis=0).T[:WIDTH]
    lane = lanes(value.shape)
    row = lax.broadcasted_iota(jnp.int32, value.shape, 0)
    real = jnp.where(lane >= row, value, across)
    imag = jnp.where(lane == row, 0.0, jnp.where(lane < row, value, -across))
    value = jnp.where(lane < WIDTH, real, 0.0)
    value = value + jnp.where((lane >= WIDTH) & (lane < 2 * WIDTH), pltpu.roll(imag, WIDTH, 1), 0.0)
    invert_factor(value, turn_ref)
    out = nt_dot(image_ref[...], turn_ref[...]).T
    for part in range(2):
        for block in range(2):
            start = (2 * block + part) * WIDTH
            out_ref[part, :, block * TILE : (block + 1) * TILE] = out[start : start + WIDTH]


def last_basis(image, grams):
    return pl.pallas_call(
        basis_kernel,
        out_shape=jax.ShapeDtypeStruct((2, WIDTH, 2 * TILE), jnp.float32),
        scratch_shapes=[pltpu.VMEM((TILE, TILE), jnp.float32)],
        compiler_params=pltpu.CompilerParams(vmem_limit_bytes=6 * MIB),
        name="basis",
    )(image, grams)


def along_x(value, step):
    return lax.ppermute(value, "row", [(i, (i + 2 * step) % 8) for i in range(8)])


def other_core(value):
    return lax.ppermute(value, "row", [(i, i ^ 1) for i in range(8)])


def to_column(value):
    return lax.all_to_all(value, "col", split_axis=0, concat_axis=0, tiled=True)


def gather_row(value):
    mine = jnp.stack([value] + [along_x(value, d) for d in (1, 2, 3)], 0)
    return mine, other_core(mine)


def reduce_row(value):
    half = value.shape[0] // 2
    mine = value[:half] + other_core(value[half:])
    return [mine[0:1]] + [along_x(mine[d : d + 1], d) for d in (1, 2, 3)]


def shards(tile_weight, tile_angle, tile_list, tile_count, init_basis):
    place = lax.axis_index("row")
    x_place, core = place // 2, place % 2
    weights = tile_weight.reshape(SLOTS, TILE, TILE)
    angles = tile_angle.reshape(SLOTS, TILE, TILE)
    listing = tile_list.reshape(SLOTS, 2)
    row_of = listing[:, 0] % ROW_BLOCKS
    col_global = listing[:, 1]
    piece = col_global // ROW_BLOCKS
    core_away = (piece % 2) ^ core
    col_from = (core_away * 4 + (x_place - piece // 2) % 4) * 2 + col_global % 2
    col_to = (core_away * 4 + (piece // 2 - x_place) % 4) * 2 + col_global % 2
    live = (jnp.arange(2)[None, :] < tile_count.reshape(SLOTS // 2, 1)).reshape(SLOTS).astype(jnp.int32)
    slots = jnp.arange(SLOTS, dtype=jnp.int32)
    earlier = slots[None, :] < slots[:, None]
    count = jnp.sum(live)
    live_before = jnp.sum(jnp.where(earlier, live[None, :], 0), axis=1)
    at = jnp.where(live > 0, live_before, count + slots - live_before)
    code = slots + SLOTS * (col_from + COL_BLOCKS * (col_to + COL_BLOCKS * row_of))
    code = jnp.sum(jnp.where(at[None, :] == slots[:, None], code[None, :], 0), axis=1)
    order = code % SLOTS
    takes_col = code // SLOTS % COL_BLOCKS
    puts_col = code // (SLOTS * COL_BLOCKS) % COL_BLOCKS
    rows = code // (SLOTS * COL_BLOCKS * COL_BLOCKS)
    puts_col = jnp.where(slots < count, puts_col, COL_BLOCKS)
    rows = jnp.where(slots < count, rows, ROW_BLOCKS)
    count = count.reshape(1)

    plain, turned, row_part, col_part = complex_tiles(order, rows, puts_col, count, weights, angles)
    row_part = to_column(row_part)
    col_parts = reduce_row(col_part)
    degree = jnp.sum(row_part, axis=0) + sum(c[0] for c in col_parts)
    scale = lax.rsqrt(degree[:2])
    scale = jnp.broadcast_to(scale.T[:, :, None], (TILE, 2, 2 * WIDTH)).reshape(TILE, TILE)

    basis = jnp.transpose(init_basis.reshape(2, WIDTH, 2, TILE), (3, 2, 0, 1)).reshape(TILE, TILE)
    sent = (basis * scale).astype(jnp.bfloat16)
    body, turn = sent, None
    for rounds in range(ITERS):
        near, far = gather_row(body)
        column = to_column(jnp.broadcast_to(sent[None], (16, TILE, TILE)))
        forward = products(
            1.0, takes_col, rows, count, plain, [near, far], (16, body.shape[0], TILE), True, "forward"
        )
        mirror = products(
            -1.0, rows, puts_col, count, turned, [column], (8, TILE, TILE), False, "mirror"
        )
        wide = to_column(forward)
        parts = reduce_row(mirror)
        if rounds > 0:
            turn = turn_of(wide)
        sent, body = new_image(wide, parts, scale, turn, rounds == ITERS - 1)
    grams = jnp.broadcast_to(body, (128, 8, TILE))
    grams = lax.all_to_all(grams, ("row", "col"), split_axis=0, concat_axis=0, tiled=True)
    return last_basis(sent, grams)


def solution(mesh):
    placed = (
        P(("row", "col"), None, None, None, None),
        P(("row", "col"), None, None, None, None),
        P(("row", "col"), None, None, None),
        P(("row", "col"), None),
        P(None, None, ("row", "col")),
    )
    return jax.shard_map(
        shards, mesh=mesh, in_specs=placed, out_specs=P(None, None, ("row", "col")), check_vma=False
    )
```

```python
import functools

import jax
import jax.numpy as jnp
from jax import lax
from jax.experimental import pallas as pl
from jax.experimental.pallas import tpu as pltpu
from jax.sharding import PartitionSpec as P

ITERS = 3
IMAGES = 32768
TILE = 128
WIDTH = 32
SLOTS = 256
ROW_BLOCKS = 32
COL_BLOCKS = 16
CHUNK = 16
TRIG_CHUNK = 8
HALF_SIN = (0.5, -0.020833322778344154, 0.00026040783268399537, -1.5475804957532091e-06, 5.088141019626846e-09)
HALF_COS = (0.9999999403953552, -0.1249997615814209, 0.0026039734948426485, -2.164632678613998e-05, 9.044046578310372e-08)
HIGHEST = lax.Precision.HIGHEST
MIB = 1 << 20


def horner(u, coefs):
    value = coefs[-1]
    for coef in coefs[-2::-1]:
        value = value * u + coef
    return value


def lanes(shape):
    return lax.broadcasted_iota(jnp.int32, shape, 1)


def pair_swap(x):
    even = (lanes(x.shape) // WIDTH) % 2 == 0
    return jnp.where(even, -pltpu.roll(x, TILE - WIDTH, 1), pltpu.roll(x, WIDTH, 1))


VECTOR = pl.BlockSpec(memory_space=pltpu.VMEM)
SCALAR = pl.BlockSpec(memory_space=pltpu.SMEM)


FAR = pl.BlockSpec(memory_space=pl.ANY)


def fetch(source, target, sems, c):
    part = pl.ds(c * CHUNK, CHUNK)
    return pltpu.make_async_copy(source.at[part], target.at[part], sems.at[c])


def start_fetches(source, target, sems, chunks):
    def start(c, carry):
        fetch(source, target, sems, c).start()
        return carry

    lax.fori_loop(0, chunks, start, 0)


def tiles_kernel(
    order, rows, cols, count, far_w, far_a, far_plain, far_turned, row_ref, col_ref,
    w_ref, a_ref, plain, turned, row_acc, col_acc, w_sems, a_sems, out_sems,
):
    def start(c, carry):
        fetch(far_w, w_ref, w_sems, c).start()
        fetch(far_a, a_ref, a_sems, c).start()
        return carry

    lax.fori_loop(0, SLOTS // CHUNK, start, 0)
    row_acc[...] = jnp.zeros_like(row_acc)
    col_acc[...] = jnp.zeros_like(col_acc)
    chunks = pl.cdiv(count[0], CHUNK) * (CHUNK // TRIG_CHUNK)

    def outgoing(c):
        part = pl.ds(c * TRIG_CHUNK, TRIG_CHUNK)
        yield pltpu.make_async_copy(plain.at[c % 2], far_plain.at[part], out_sems.at[c % 2, 0])
        yield pltpu.make_async_copy(turned.at[c % 2], far_turned.at[part], out_sems.at[c % 2, 1])

    def arrive(c, carry):
        fetch(far_w, w_ref, w_sems, c).wait()
        fetch(far_a, a_ref, a_sems, c).wait()
        return carry

    def step(c, here):
        reach = order[c * TRIG_CHUNK + TRIG_CHUNK - 1] // CHUNK + 1
        need = jnp.where(c >= chunks - CHUNK // TRIG_CHUNK, SLOTS // CHUNK, reach)
        lax.fori_loop(here, need, arrive, 0)

        @pl.when(c >= 2)
        def _():
            for copy in outgoing(c - 2):
                copy.wait()

        side = c % 2
        for u in range(TRIG_CHUNK):
            slot = c * TRIG_CHUNK + u
            source = order[slot]
            theta = a_ref[source].astype(jnp.float32)
            w = w_ref[source].astype(jnp.float32)
            square = theta * theta
            sine = theta * horner(square, HALF_SIN)
            cosine = horner(square, HALF_COS)
            part = w * sine
            real = (0.5 * w - part * sine).astype(jnp.bfloat16)
            imag = (part * cosine).astype(jnp.bfloat16)
            plain[side, u, :, :TILE] = real
            plain[side, u, :, TILE:] = imag
            turned[side, u, :, :TILE] = real.T
            turned[side, u, :, TILE:] = imag.T
            row_acc[rows[slot]] += w
            col_acc[cols[slot]] += jnp.sum(w.reshape(TILE // 8, 8, TILE), axis=0)
        for copy in outgoing(c):
            copy.start()
        return need

    lax.fori_loop(0, chunks, step, 0)
    for p in range(ROW_BLOCKS // 2):
        sums = [jnp.sum(row_acc[2 * p + k].T, axis=0, keepdims=True) for k in range(2)]
        row_ref[p] = 0.5 * jnp.concatenate(sums * 4, axis=0)
    for p in range(COL_BLOCKS // 2):
        sums = [jnp.sum(col_acc[2 * p + k], axis=0, keepdims=True) for k in range(2)]
        col_ref[p] = 0.5 * jnp.concatenate(sums * 4, axis=0)
    for back in (2, 1):
        for copy in outgoing(chunks - back):
            copy.wait()


def complex_tiles(order, rows, cols, count, weights, angles):
    return pl.pallas_call(
        tiles_kernel,
        in_specs=[SCALAR] * 4 + [FAR, FAR],
        out_specs=[FAR, FAR, VECTOR, VECTOR],
        out_shape=[jax.ShapeDtypeStruct((SLOTS, TILE, 2 * TILE), jnp.bfloat16)] * 2
        + [
            jax.ShapeDtypeStruct((ROW_BLOCKS // 2, 8, TILE), jnp.float32),
            jax.ShapeDtypeStruct((COL_BLOCKS // 2, 8, TILE), jnp.float32),
        ],
        scratch_shapes=[
            pltpu.VMEM((SLOTS, TILE, TILE), jnp.bfloat16),
            pltpu.VMEM((SLOTS, TILE, TILE), jnp.bfloat16),
            pltpu.VMEM((2, TRIG_CHUNK, TILE, 2 * TILE), jnp.bfloat16),
            pltpu.VMEM((2, TRIG_CHUNK, TILE, 2 * TILE), jnp.bfloat16),
            pltpu.VMEM((ROW_BLOCKS + 1, TILE, TILE), jnp.float32),
            pltpu.VMEM((COL_BLOCKS + 1, 8, TILE), jnp.float32),
            pltpu.SemaphoreType.DMA((SLOTS // CHUNK,)),
            pltpu.SemaphoreType.DMA((SLOTS // CHUNK,)),
            pltpu.SemaphoreType.DMA((2, 2)),
        ],
        compiler_params=pltpu.CompilerParams(vmem_limit_bytes=58 * MIB),
        cost_estimate=pl.CostEstimate(flops=0, bytes_accessed=50 * MIB, transcendentals=0),
        name="complex_tiles",
    )(order, rows, cols, count, weights, angles)


def product_kernel(sign, sizes, apart, takes, puts, count, far_ref, *refs):
    x_refs = refs[: len(sizes)]
    out_ref, x_mat, acc, tiles_ref, sems = refs[len(sizes) :][:5]
    chunks = pl.cdiv(count[0], CHUNK)
    start_fetches(far_ref, tiles_ref, sems, chunks)
    low = lanes((TILE, TILE)) < 2 * WIDTH
    acc[...] = jnp.zeros_like(acc)
    x_mat[2 * sum(sizes)] = jnp.zeros_like(x_mat[0])
    base = 0
    for x_ref, size in zip(x_refs, sizes):
        for p in range(size):
            value = x_ref[p, :TILE].astype(jnp.float32)
            high = value.astype(jnp.bfloat16).astype(jnp.float32)
            rest = value - high
            for k in range(2):
                if k == 0:
                    top = jnp.where(low, high, pltpu.roll(rest, 2 * WIDTH, 1))
                else:
                    top = jnp.where(low, pltpu.roll(high, 2 * WIDTH, 1), rest)
                x_mat[base + 2 * p + k, :TILE] = top.astype(jnp.bfloat16)
                x_mat[base + 2 * p + k, TILE:] = (sign * pair_swap(top)).astype(jnp.bfloat16)
        base += 2 * size

    def add(c, size):
        for part in range(size):
            fetch(far_ref, tiles_ref, sems, c + part).wait()
        for u in range(CHUNK * size):
            slot = c * CHUNK + u
            acc[puts[slot]] += jnp.dot(
                tiles_ref[slot], x_mat[takes[slot]], preferred_element_type=jnp.float32
            )

    def step(c, carry):
        add(2 * c, 2)
        return carry

    lax.fori_loop(0, chunks // 2, step, 0)

    @pl.when(chunks % 2 == 1)
    def _():
        add(chunks - 1, 1)

    near, out_sems = refs[len(sizes) :][5:] if apart else (out_ref, None)
    if out_ref.shape[1] > TILE:
        gram = sum(x_ref[p, TILE:] for x_ref, size in zip(x_refs, sizes) for p in range(size))
    copies = []
    for p in range(out_ref.shape[0]):
        if out_ref.shape[1] > TILE:
            near[p, TILE:] = gram
        first, second = acc[2 * p], acc[2 * p + 1]
        near[p, :TILE] = jnp.where(
            low,
            first + pltpu.roll(first, 2 * WIDTH, 1),
            second + pltpu.roll(second, 2 * WIDTH, 1),
        )
        if apart:
            copies.append(pltpu.make_async_copy(near.at[p], out_ref.at[p], out_sems.at[p]))
            copies[-1].start()
    for copy in copies:
        copy.wait()


def products(sign, takes, puts, count, tiles, sources, out_shape, apart, name):
    sizes = tuple(s.shape[0] for s in sources)
    scratch = [
        pltpu.VMEM((2 * sum(sizes) + 1, 2 * TILE, TILE), jnp.bfloat16),
        pltpu.VMEM((2 * out_shape[0] + 1, TILE, TILE), jnp.float32),
        pltpu.VMEM((SLOTS, TILE, 2 * TILE), jnp.bfloat16),
        pltpu.SemaphoreType.DMA((SLOTS // CHUNK,)),
    ]
    if apart:
        scratch += [pltpu.VMEM(out_shape, jnp.float32), pltpu.SemaphoreType.DMA((out_shape[0],))]
    return pl.pallas_call(
        functools.partial(product_kernel, sign, sizes, apart),
        in_specs=[SCALAR, SCALAR, SCALAR, FAR] + [VECTOR] * len(sources),
        out_specs=FAR if apart else VECTOR,
        scratch_shapes=scratch,
        out_shape=jax.ShapeDtypeStruct(out_shape, jnp.float32),
        compiler_params=pltpu.CompilerParams(vmem_limit_bytes=52 * MIB),
        cost_estimate=pl.CostEstimate(flops=0, bytes_accessed=30 * MIB, transcendentals=0),
        name=name,
    )(takes, puts, count, tiles, *sources)


def gather_kernel(turned, final, n_parts, *refs):
    wide_ref, part_refs = refs[0], refs[1 : 1 + n_parts]
    scale_ref = refs[1 + n_parts]
    rest = refs[2 + n_parts :]
    total = wide_ref[0, :TILE]
    for p in range(1, wide_ref.shape[0]):
        total = total + wide_ref[p, :TILE]
    for ref in part_refs:
        total = total + ref[0]
    scale = scale_ref[...]
    image = total * scale
    if turned:
        image = nt_dot(image, rest[0][...])
        rest = rest[1:]
    across = image.T
    gram = nt_dot(across, across)
    pairs = gram[: 2 * WIDTH] + pltpu.roll(gram[2 * WIDTH :], 2 * WIDTH, 1)
    upper, lower = pairs[:WIDTH], pairs[WIDTH:]
    lane = lanes(upper.shape)
    other = jnp.where(lane < WIDTH, pltpu.roll(lower, TILE - WIDTH, 1), -pltpu.roll(lower, WIDTH, 1))
    both = upper + other
    if final:
        image_ref, gram_ref = rest
        image_ref[...] = image
        row = lax.broadcasted_iota(jnp.int32, upper.shape, 0)
        packed = jnp.where(lane >= row, both, pltpu.roll(both, TILE - WIDTH, 1))
        out = packed[:8]
        group = lanes((8, TILE)) // WIDTH
        for g in range(1, 4):
            out = jnp.where(group == g, pltpu.roll(packed[8 * g : 8 * g + 8], WIDTH * g, 1), out)
        gram_ref[0] = out
    else:
        sent_ref, body_ref = rest
        value = image * scale
        sent_ref[...] = value
        body_ref[:TILE] = value
        low = lanes((WIDTH // 2, TILE)) < 2 * WIDTH
        body_ref[TILE:] = jnp.where(
            low, both[: WIDTH // 2], pltpu.roll(both[WIDTH // 2 :], 2 * WIDTH, 1)
        )


def nt_dot(left, right):
    return lax.dot_general(
        left, right, (((1,), (1,)), ((), ())), precision=HIGHEST, preferred_element_type=jnp.float32
    )


def new_image(wide, parts, scale, turn, final):
    operands = [wide, *parts, scale] + ([] if turn is None else [turn])
    second = (1, 8, TILE) if final else (TILE + WIDTH // 2, TILE)
    return pl.pallas_call(
        functools.partial(gather_kernel, turn is not None, final, len(parts)),
        out_shape=[
            jax.ShapeDtypeStruct((TILE, TILE), jnp.float32),
            jax.ShapeDtypeStruct(second, jnp.float32),
        ],
        compiler_params=pltpu.CompilerParams(vmem_limit_bytes=6 * MIB),
        cost_estimate=pl.CostEstimate(flops=0, bytes_accessed=6 * MIB, transcendentals=0),
        name="new_image",
    )(*operands)


def spread(x, lane):
    return jnp.broadcast_to(x[:, lane : lane + 1], (8, TILE))


def invert_factor(value, turn_ref):
    size = 4
    lane = lanes((WIDTH, TILE))
    place = lax.broadcasted_iota(jnp.int32, (WIDTH, TILE), 0)
    diagonal = lane == place
    trace = jnp.sum(jnp.where(diagonal, value, 0.0))
    ridge = 0.01 * trace / WIDTH + 1e-6
    value = value + jnp.where(diagonal, ridge, 0.0)
    value = value + jnp.where(lane == place + 2 * WIDTH, 1.0, 0.0)
    groups = [value[8 * g : 8 * g + 8] for g in range(4)]
    within = lax.broadcasted_iota(jnp.int32, (8, TILE), 0)
    for c in range(0, WIDTH, size):
        g, o = c // 8, c % 8
        rows = [jnp.broadcast_to(groups[g][o + r : o + r + 1], (8, TILE)) for r in range(size)]
        turned = [pair_swap(row) for row in rows]
        block = {
            (r, k): (spread(rows[r], c + k), spread(rows[r], WIDTH + c + k))
            for r in range(size)
            for k in range(r, size)
        }
        below = list(range(g if o + size < 8 else g + 1, 4))
        cols = {
            (h, k): (spread(groups[h], c + k), spread(groups[h], WIDTH + c + k))
            for h in below
            for k in range(size)
        }
        new = {h: groups[h] for h in below}
        for k in range(size):
            inverse = 1.0 / block[k, k][0]
            for r in range(k + 1, size):
                real, imag = block[k, r][0] * inverse, -block[k, r][1] * inverse
                rows[r], turned[r] = (
                    rows[r] - (real * rows[k] + imag * turned[k]),
                    turned[r] - (real * turned[k] - imag * rows[k]),
                )
                for j in range(r, size):
                    other = block[k, j]
                    block[r, j] = (
                        block[r, j][0] - (real * other[0] - imag * other[1]),
                        block[r, j][1] - (real * other[1] + imag * other[0]),
                    )
            for h in below:
                real, imag = cols[h, k][0] * inverse, cols[h, k][1] * inverse
                for j in range(k + 1, size):
                    other = block[k, j]
                    cols[h, j] = (
                        cols[h, j][0] - (real * other[0] - imag * other[1]),
                        cols[h, j][1] - (real * other[1] + imag * other[0]),
                    )
                step = real * rows[k] + imag * turned[k]
                new[h] = new[h] - (jnp.where(within >= o + size, step, 0.0) if h == g else step)
        kept = new.get(g, groups[g])
        for r in range(size):
            kept = jnp.where(within == o + r, rows[r], kept)
        for h in below:
            groups[h] = new[h]
        groups[g] = kept
    value = jnp.concatenate(groups, axis=0)
    pivot = jnp.sum(jnp.where(diagonal, value, 0.0), axis=1, keepdims=True)
    value = value * lax.rsqrt(pivot)
    second = jnp.where(lane >= 2 * WIDTH, value, 0.0)
    first = pltpu.roll(second, 2 * WIDTH, 1)
    turn_ref[0:WIDTH] = first
    turn_ref[WIDTH : 2 * WIDTH] = pair_swap(first)
    turn_ref[2 * WIDTH : 3 * WIDTH] = second
    turn_ref[3 * WIDTH :] = pair_swap(second)


def turn_kernel(wide_ref, turn_ref):
    packed = wide_ref[0, TILE:]
    for p in range(1, wide_ref.shape[0]):
        packed = packed + wide_ref[p, TILE:]
    packed = packed * (1.0 / IMAGES)
    value = jnp.concatenate([packed, pltpu.roll(packed, 2 * WIDTH, 1)], axis=0)
    invert_factor(jnp.where(lanes(value.shape) < 2 * WIDTH, value, 0.0), turn_ref)


def turn_of(wide):
    return pl.pallas_call(
        turn_kernel,
        out_shape=jax.ShapeDtypeStruct((TILE, TILE), jnp.float32),
        compiler_params=pltpu.CompilerParams(vmem_limit_bytes=6 * MIB),
        cost_estimate=pl.CostEstimate(flops=0, bytes_accessed=6 * MIB, transcendentals=0),
        name="turn",
    )(wide)


def basis_kernel(image_ref, gram_ref, out_ref, turn_ref):
    packed = jnp.sum(gram_ref[...], axis=0) * (1.0 / IMAGES)
    value = jnp.concatenate(
        [packed] + [pltpu.roll(packed, TILE - WIDTH * g, 1) for g in range(1, 4)], axis=0
    )
    across = jnp.concatenate([value] + [jnp.zeros_like(value)] * 3, axis=0).T[:WIDTH]
    lane = lanes(value.shape)
    row = lax.broadcasted_iota(jnp.int32, value.shape, 0)
    real = jnp.where(lane >= row, value, across)
    imag = jnp.where(lane == row, 0.0, jnp.where(lane < row, value, -across))
    value = jnp.where(lane < WIDTH, real, 0.0)
    value = value + jnp.where((lane >= WIDTH) & (lane < 2 * WIDTH), pltpu.roll(imag, WIDTH, 1), 0.0)
    invert_factor(value, turn_ref)
    out = nt_dot(image_ref[...], turn_ref[...]).T
    for part in range(2):
        for block in range(2):
            start = (2 * block + part) * WIDTH
            out_ref[part, :, block * TILE : (block + 1) * TILE] = out[start : start + WIDTH]


def last_basis(image, grams):
    return pl.pallas_call(
        basis_kernel,
        out_shape=jax.ShapeDtypeStruct((2, WIDTH, 2 * TILE), jnp.float32),
        scratch_shapes=[pltpu.VMEM((TILE, TILE), jnp.float32)],
        compiler_params=pltpu.CompilerParams(vmem_limit_bytes=6 * MIB),
        name="basis",
    )(image, grams)


def along_x(value, step):
    return lax.ppermute(value, "row", [(i, (i + 2 * step) % 8) for i in range(8)])


def other_core(value):
    return lax.ppermute(value, "row", [(i, i ^ 1) for i in range(8)])


def to_column(value):
    return lax.all_to_all(value, "col", split_axis=0, concat_axis=0, tiled=True)


def gather_row(value):
    mine = jnp.stack([value] + [along_x(value, d) for d in (1, 2, 3)], 0)
    return mine, other_core(mine)


def reduce_row(value):
    half = value.shape[0] // 2
    mine = value[:half] + other_core(value[half:])
    return [mine[0:1]] + [along_x(mine[d : d + 1], d) for d in (1, 2, 3)]


def shards(tile_weight, tile_angle, tile_list, tile_count, init_basis):
    place = lax.axis_index("row")
    x_place, core = place // 2, place % 2
    weights = tile_weight.reshape(SLOTS, TILE, TILE)
    angles = tile_angle.reshape(SLOTS, TILE, TILE)
    listing = tile_list.reshape(SLOTS, 2)
    row_of = listing[:, 0] % ROW_BLOCKS
    col_global = listing[:, 1]
    piece = col_global // ROW_BLOCKS
    core_away = (piece % 2) ^ core
    col_from = (core_away * 4 + (x_place - piece // 2) % 4) * 2 + col_global % 2
    col_to = (core_away * 4 + (piece // 2 - x_place) % 4) * 2 + col_global % 2
    live = (jnp.arange(2)[None, :] < tile_count.reshape(SLOTS // 2, 1)).reshape(SLOTS).astype(jnp.int32)
    slots = jnp.arange(SLOTS, dtype=jnp.int32)
    earlier = slots[None, :] < slots[:, None]
    count = jnp.sum(live)
    live_before = jnp.sum(jnp.where(earlier, live[None, :], 0), axis=1)
    at = jnp.where(live > 0, live_before, count + slots - live_before)
    code = slots + SLOTS * (col_from + COL_BLOCKS * (col_to + COL_BLOCKS * row_of))
    code = jnp.sum(jnp.where(at[None, :] == slots[:, None], code[None, :], 0), axis=1)
    order = code % SLOTS
    takes_col = code // SLOTS % COL_BLOCKS
    puts_col = code // (SLOTS * COL_BLOCKS) % COL_BLOCKS
    rows = code // (SLOTS * COL_BLOCKS * COL_BLOCKS)
    puts_col = jnp.where(slots < count, puts_col, COL_BLOCKS)
    rows = jnp.where(slots < count, rows, ROW_BLOCKS)
    count = count.reshape(1)

    plain, turned, row_part, col_part = complex_tiles(order, rows, puts_col, count, weights, angles)
    row_part = to_column(row_part)
    col_parts = reduce_row(col_part)
    degree = jnp.sum(row_part, axis=0) + sum(c[0] for c in col_parts)
    scale = lax.rsqrt(degree[:2])
    scale = jnp.broadcast_to(scale.T[:, :, None], (TILE, 2, 2 * WIDTH)).reshape(TILE, TILE)

    basis = jnp.transpose(init_basis.reshape(2, WIDTH, 2, TILE), (3, 2, 0, 1)).reshape(TILE, TILE)
    sent = (basis * scale).astype(jnp.bfloat16)
    body, turn = sent, None
    for rounds in range(ITERS):
        near, far = gather_row(body)
        column = to_column(jnp.broadcast_to(sent[None], (16, TILE, TILE)))
        forward = products(
            1.0, takes_col, rows, count, plain, [near, far], (16, body.shape[0], TILE), True, "forward"
        )
        mirror = products(
            -1.0, rows, puts_col, count, turned, [column], (8, TILE, TILE), False, "mirror"
        )
        wide = to_column(forward)
        parts = reduce_row(mirror)
        if rounds > 0:
            turn = turn_of(wide)
        sent, body = new_image(wide, parts, scale, turn, rounds == ITERS - 1)
    body = body + other_core(body)
    grams = lax.all_to_all(
        jnp.broadcast_to(body, (64, 8, TILE)),
        ("row", "col"),
        split_axis=0,
        concat_axis=0,
        tiled=True,
        axis_index_groups=[[16 * r + c for r in range(core, 8, 2) for c in range(16)] for core in (0, 1)],
    )
    return last_basis(sent, grams)


def solution(mesh):
    placed = (
        P(("row", "col"), None, None, None, None),
        P(("row", "col"), None, None, None, None),
        P(("row", "col"), None, None, None),
        P(("row", "col"), None),
        P(None, None, ("row", "col")),
    )
    return jax.shard_map(
        shards, mesh=mesh, in_specs=placed, out_specs=P(None, None, ("row", "col")), check_vma=False
    )
```

```python
import functools

import jax
import jax.numpy as jnp
from jax import lax
from jax.experimental import pallas as pl
from jax.experimental.pallas import tpu as pltpu
from jax.sharding import PartitionSpec as P

ITERS = 3
IMAGES = 32768
TILE = 128
WIDTH = 32
SLOTS = 256
ROW_BLOCKS = 32
COL_BLOCKS = 16
CHUNK = 16
TRIG_CHUNK = 16
HALF_SIN = (0.5, -0.020833322778344154, 0.00026040783268399537, -1.5475804957532091e-06, 5.088141019626846e-09)
HALF_COS = (0.9999999403953552, -0.1249997615814209, 0.0026039734948426485, -2.164632678613998e-05, 9.044046578310372e-08)
HIGHEST = lax.Precision.HIGHEST
MIB = 1 << 20


def horner(u, coefs):
    value = coefs[-1]
    for coef in coefs[-2::-1]:
        value = value * u + coef
    return value


def lanes(shape):
    return lax.broadcasted_iota(jnp.int32, shape, 1)


def pair_swap(x):
    even = (lanes(x.shape) // WIDTH) % 2 == 0
    return jnp.where(even, -pltpu.roll(x, TILE - WIDTH, 1), pltpu.roll(x, WIDTH, 1))


VECTOR = pl.BlockSpec(memory_space=pltpu.VMEM)
SCALAR = pl.BlockSpec(memory_space=pltpu.SMEM)


FAR = pl.BlockSpec(memory_space=pl.ANY)


def fetch(source, target, sems, c):
    part = pl.ds(c * CHUNK, CHUNK)
    return pltpu.make_async_copy(source.at[part], target.at[part], sems.at[c])


def start_fetches(source, target, sems, chunks):
    def start(c, carry):
        fetch(source, target, sems, c).start()
        return carry

    lax.fori_loop(0, chunks, start, 0)


def tiles_kernel(
    order, rows, cols, count, far_w, far_a, far_plain, far_turned, row_ref, own_ref, other_ref,
    w_ref, a_ref, plain, turned, row_acc, col_acc, w_sems, a_sems, out_sems,
):
    def start(c, carry):
        fetch(far_w, w_ref, w_sems, c).start()
        fetch(far_a, a_ref, a_sems, c).start()
        return carry

    lax.fori_loop(0, SLOTS // CHUNK, start, 0)
    row_acc[...] = jnp.zeros_like(row_acc)
    col_acc[...] = jnp.zeros_like(col_acc)
    chunks = pl.cdiv(count[0], CHUNK) * (CHUNK // TRIG_CHUNK)

    def outgoing(c):
        part = pl.ds(c * TRIG_CHUNK, TRIG_CHUNK)
        yield pltpu.make_async_copy(plain.at[c % 2], far_plain.at[part], out_sems.at[c % 2, 0])
        yield pltpu.make_async_copy(turned.at[c % 2], far_turned.at[part], out_sems.at[c % 2, 1])

    def arrive(c, carry):
        fetch(far_w, w_ref, w_sems, c).wait()
        fetch(far_a, a_ref, a_sems, c).wait()
        return carry

    def step(c, here):
        reach = order[c * TRIG_CHUNK + TRIG_CHUNK - 1] // CHUNK + 1
        need = jnp.where(c >= chunks - CHUNK // TRIG_CHUNK, SLOTS // CHUNK, reach)
        lax.fori_loop(here, need, arrive, 0)

        @pl.when(c >= 2)
        def _():
            for copy in outgoing(c - 2):
                copy.wait()

        side = c % 2
        for u in range(TRIG_CHUNK):
            slot = c * TRIG_CHUNK + u
            source = order[slot]
            theta = a_ref[source].astype(jnp.float32)
            w = w_ref[source].astype(jnp.float32)
            square = theta * theta
            sine = theta * horner(square, HALF_SIN)
            cosine = horner(square, HALF_COS)
            part = w * sine
            real = (0.5 * w - part * sine).astype(jnp.bfloat16)
            imag = (part * cosine).astype(jnp.bfloat16)
            plain[side, u, :, :TILE] = real
            plain[side, u, :, TILE:] = imag
            turned[side, u, :, :TILE] = real.T
            turned[side, u, :, TILE:] = imag.T
            row_acc[rows[slot]] += w
            col_acc[cols[slot]] += jnp.sum(w.reshape(TILE // 8, 8, TILE), axis=0)
        for copy in outgoing(c):
            copy.start()
        return need

    lax.fori_loop(0, chunks, step, 0)
    for p in range(ROW_BLOCKS // 2):
        sums = [jnp.sum(row_acc[2 * p + k].T, axis=0, keepdims=True) for k in range(2)]
        row_ref[p] = 0.5 * jnp.concatenate(sums * 4, axis=0)
    for p in range(COL_BLOCKS // 2):
        sums = [jnp.sum(col_acc[2 * p + k], axis=0, keepdims=True) for k in range(2)]
        col_ref = own_ref if p < 4 else other_ref
        col_ref[p % 4] = 0.5 * jnp.concatenate(sums * 4, axis=0)

    @pl.when(chunks >= 2)
    def _():
        for copy in outgoing(chunks - 2):
            copy.wait()

    for copy in outgoing(chunks - 1):
        copy.wait()


def complex_tiles(order, rows, cols, count, weights, angles):
    return pl.pallas_call(
        tiles_kernel,
        in_specs=[SCALAR] * 4 + [FAR, FAR],
        out_specs=[FAR, FAR, VECTOR, VECTOR, VECTOR],
        out_shape=[jax.ShapeDtypeStruct((SLOTS, TILE, 2 * TILE), jnp.bfloat16)] * 2
        + [
            jax.ShapeDtypeStruct((ROW_BLOCKS // 2, 8, TILE), jnp.float32),
            jax.ShapeDtypeStruct((COL_BLOCKS // 4, 8, TILE), jnp.float32),
            jax.ShapeDtypeStruct((COL_BLOCKS // 4, 8, TILE), jnp.float32),
        ],
        scratch_shapes=[
            pltpu.VMEM((SLOTS, TILE, TILE), jnp.bfloat16),
            pltpu.VMEM((SLOTS, TILE, TILE), jnp.bfloat16),
            pltpu.VMEM((2, TRIG_CHUNK, TILE, 2 * TILE), jnp.bfloat16),
            pltpu.VMEM((2, TRIG_CHUNK, TILE, 2 * TILE), jnp.bfloat16),
            pltpu.VMEM((ROW_BLOCKS + 1, TILE, TILE), jnp.float32),
            pltpu.VMEM((COL_BLOCKS + 1, 8, TILE), jnp.float32),
            pltpu.SemaphoreType.DMA((SLOTS // CHUNK,)),
            pltpu.SemaphoreType.DMA((SLOTS // CHUNK,)),
            pltpu.SemaphoreType.DMA((2, 2)),
        ],
        compiler_params=pltpu.CompilerParams(vmem_limit_bytes=58 * MIB),
        cost_estimate=pl.CostEstimate(flops=0, bytes_accessed=50 * MIB, transcendentals=0),
        name="complex_tiles",
    )(order, rows, cols, count, weights, angles)


def product_kernel(sign, sizes, apart, takes, puts, count, far_ref, *refs):
    x_refs = refs[: len(sizes)]
    out_ref, x_mat, acc, tiles_ref, sems = refs[len(sizes) :][:5]
    chunks = pl.cdiv(count[0], CHUNK)
    start_fetches(far_ref, tiles_ref, sems, chunks)
    low = lanes((TILE, TILE)) < 2 * WIDTH
    acc[...] = jnp.zeros_like(acc)
    x_mat[2 * sum(sizes)] = jnp.zeros_like(x_mat[0])
    base = 0
    for x_ref, size in zip(x_refs, sizes):
        for p in range(size):
            value = x_ref[p, :TILE].astype(jnp.float32)
            high = value.astype(jnp.bfloat16).astype(jnp.float32)
            rest = value - high
            for k in range(2):
                if k == 0:
                    top = jnp.where(low, high, pltpu.roll(rest, 2 * WIDTH, 1))
                else:
                    top = jnp.where(low, pltpu.roll(high, 2 * WIDTH, 1), rest)
                x_mat[base + 2 * p + k, :TILE] = top.astype(jnp.bfloat16)
                x_mat[base + 2 * p + k, TILE:] = (sign * pair_swap(top)).astype(jnp.bfloat16)
        base += 2 * size

    def add(c, size):
        for part in range(size):
            fetch(far_ref, tiles_ref, sems, c + part).wait()
        for u in range(CHUNK * size):
            slot = c * CHUNK + u
            acc[puts[slot]] += jnp.dot(
                tiles_ref[slot], x_mat[takes[slot]], preferred_element_type=jnp.float32
            )

    def step(c, carry):
        add(2 * c, 2)
        return carry

    lax.fori_loop(0, chunks // 2, step, 0)

    @pl.when(chunks % 2 == 1)
    def _():
        add(chunks - 1, 1)

    near, out_sems = refs[len(sizes) :][5:] if apart else (out_ref, None)
    if out_ref.shape[1] > TILE:
        gram = sum(x_ref[p, TILE:] for x_ref, size in zip(x_refs, sizes) for p in range(size))
    copies = []
    for p in range(out_ref.shape[0]):
        if out_ref.shape[1] > TILE:
            near[p, TILE:] = gram
        first, second = acc[2 * p], acc[2 * p + 1]
        near[p, :TILE] = jnp.where(
            low,
            first + pltpu.roll(first, 2 * WIDTH, 1),
            second + pltpu.roll(second, 2 * WIDTH, 1),
        )
        if apart:
            copies.append(pltpu.make_async_copy(near.at[p], out_ref.at[p], out_sems.at[p]))
            copies[-1].start()
    for copy in copies:
        copy.wait()


def products(sign, takes, puts, count, tiles, sources, out_shape, apart, name):
    sizes = tuple(s.shape[0] for s in sources)
    scratch = [
        pltpu.VMEM((2 * sum(sizes) + 1, 2 * TILE, TILE), jnp.bfloat16),
        pltpu.VMEM((2 * out_shape[0] + 1, TILE, TILE), jnp.float32),
        pltpu.VMEM((SLOTS, TILE, 2 * TILE), jnp.bfloat16),
        pltpu.SemaphoreType.DMA((SLOTS // CHUNK,)),
    ]
    if apart:
        scratch += [pltpu.VMEM(out_shape, jnp.float32), pltpu.SemaphoreType.DMA((out_shape[0],))]
    return pl.pallas_call(
        functools.partial(product_kernel, sign, sizes, apart),
        in_specs=[SCALAR, SCALAR, SCALAR, FAR] + [VECTOR] * len(sources),
        out_specs=FAR if apart else VECTOR,
        scratch_shapes=scratch,
        out_shape=jax.ShapeDtypeStruct(out_shape, jnp.float32),
        compiler_params=pltpu.CompilerParams(vmem_limit_bytes=52 * MIB),
        cost_estimate=pl.CostEstimate(flops=0, bytes_accessed=30 * MIB, transcendentals=0),
        name=name,
    )(takes, puts, count, tiles, *sources)


def gather_kernel(turned, final, n_parts, *refs):
    wide_ref, part_refs = refs[0], refs[1 : 1 + n_parts]
    scale_ref = refs[1 + n_parts]
    rest = refs[2 + n_parts :]
    total = wide_ref[0, :TILE]
    for p in range(1, wide_ref.shape[0]):
        total = total + wide_ref[p, :TILE]
    for ref in part_refs:
        total = total + ref[0]
    scale = scale_ref[...]
    image = total * scale
    if turned:
        image = nt_dot(image, rest[0][...])
        rest = rest[1:]
    copies = []
    if not final:
        body_ref, far_ref, sems = rest
        body_ref[:TILE] = image * scale
        copies = spread_copies(body_ref.at[pl.ds(0, TILE)], far_ref, sems)
    across = image.T
    gram = nt_dot(across, across)
    pairs = gram[: 2 * WIDTH] + pltpu.roll(gram[2 * WIDTH :], 2 * WIDTH, 1)
    upper, lower = pairs[:WIDTH], pairs[WIDTH:]
    lane = lanes(upper.shape)
    other = jnp.where(lane < WIDTH, pltpu.roll(lower, TILE - WIDTH, 1), -pltpu.roll(lower, WIDTH, 1))
    both = upper + other
    if final:
        image_ref, gram_ref = rest
        image_ref[...] = image
        row = lax.broadcasted_iota(jnp.int32, upper.shape, 0)
        packed = jnp.where(lane >= row, both, pltpu.roll(both, TILE - WIDTH, 1))
        out = packed[:8]
        group = lanes((8, TILE)) // WIDTH
        for g in range(1, 4):
            out = jnp.where(group == g, pltpu.roll(packed[8 * g : 8 * g + 8], WIDTH * g, 1), out)
        gram_ref[0] = out
    else:
        low = lanes((WIDTH // 2, TILE)) < 2 * WIDTH
        body_ref[TILE:] = jnp.where(
            low, both[: WIDTH // 2], pltpu.roll(both[WIDTH // 2 :], 2 * WIDTH, 1)
        )
    for copy in copies:
        copy.wait()


def spread_copies(source, target, sems):
    copies = [pltpu.make_async_copy(source, target.at[p], sems.at[p]) for p in range(16)]
    for copy in copies:
        copy.start()
    return copies


def first_kernel(n_parts, *refs):
    wide_ref, part_refs = refs[0], refs[1 : 1 + n_parts]
    basis_ref, scale_ref, sent_ref, far_ref, sems = refs[1 + n_parts :]
    degree = wide_ref[0]
    for p in range(1, wide_ref.shape[0]):
        degree = degree + wide_ref[p]
    for ref in part_refs:
        degree = degree + ref[0]
    factor = lax.rsqrt(degree)
    row = lax.broadcasted_iota(jnp.int32, (TILE, TILE), 0)
    scale = jnp.where(row < 2 * WIDTH, factor[0:1], factor[1:2]).T
    scale_ref[...] = scale
    sent_ref[...] = (basis_ref[...] * scale).astype(jnp.bfloat16)
    for copy in spread_copies(sent_ref, far_ref, sems):
        copy.wait()


def first_block(wide, parts, basis):
    return pl.pallas_call(
        functools.partial(first_kernel, len(parts)),
        in_specs=[VECTOR] * (len(parts) + 2),
        out_specs=[VECTOR, VECTOR, FAR],
        out_shape=[
            jax.ShapeDtypeStruct((TILE, TILE), jnp.float32),
            jax.ShapeDtypeStruct((TILE, TILE), jnp.bfloat16),
            jax.ShapeDtypeStruct((16, TILE, TILE), jnp.bfloat16),
        ],
        scratch_shapes=[pltpu.SemaphoreType.DMA((16,))],
        compiler_params=pltpu.CompilerParams(vmem_limit_bytes=6 * MIB),
        cost_estimate=pl.CostEstimate(flops=0, bytes_accessed=6 * MIB, transcendentals=0),
        name="first_block",
    )(wide, *parts, basis)


def nt_dot(left, right):
    return lax.dot_general(
        left, right, (((1,), (1,)), ((), ())), precision=HIGHEST, preferred_element_type=jnp.float32
    )


def new_image(wide, parts, scale, turn, final):
    operands = [wide, *parts, scale] + ([] if turn is None else [turn])
    if final:
        shapes = [(TILE, TILE), (1, 8, TILE)]
    else:
        shapes = [(TILE + WIDTH // 2, TILE), (16, TILE, TILE)]
    return pl.pallas_call(
        functools.partial(gather_kernel, turn is not None, final, len(parts)),
        in_specs=[VECTOR] * len(operands),
        out_specs=[VECTOR, VECTOR if final else FAR],
        out_shape=[jax.ShapeDtypeStruct(shape, jnp.float32) for shape in shapes],
        scratch_shapes=[] if final else [pltpu.SemaphoreType.DMA((16,))],
        compiler_params=pltpu.CompilerParams(vmem_limit_bytes=6 * MIB),
        cost_estimate=pl.CostEstimate(flops=0, bytes_accessed=6 * MIB, transcendentals=0),
        name="new_image",
    )(*operands)


def spread(x, lane):
    return jnp.broadcast_to(x[:, lane : lane + 1], (8, TILE))


def invert_factor(value, turn_ref):
    size = 4
    lane = lanes((WIDTH, TILE))
    place = lax.broadcasted_iota(jnp.int32, (WIDTH, TILE), 0)
    diagonal = lane == place
    trace = jnp.sum(jnp.where(diagonal, value, 0.0))
    ridge = 0.01 * trace / WIDTH + 1e-6
    value = value + jnp.where(diagonal, ridge, 0.0)
    value = value + jnp.where(lane == place + 2 * WIDTH, 1.0, 0.0)
    groups = [value[8 * g : 8 * g + 8] for g in range(4)]
    within = lax.broadcasted_iota(jnp.int32, (8, TILE), 0)
    for c in range(0, WIDTH, size):
        g, o = c // 8, c % 8
        rows = [jnp.broadcast_to(groups[g][o + r : o + r + 1], (8, TILE)) for r in range(size)]
        turned = [pair_swap(row) for row in rows]
        block = {
            (r, k): (spread(rows[r], c + k), spread(rows[r], WIDTH + c + k))
            for r in range(size)
            for k in range(r, size)
        }
        below = list(range(g if o + size < 8 else g + 1, 4))
        cols = {
            (h, k): (spread(groups[h], c + k), spread(groups[h], WIDTH + c + k))
            for h in below
            for k in range(size)
        }
        new = {h: groups[h] for h in below}
        for k in range(size):
            inverse = 1.0 / block[k, k][0]
            for r in range(k + 1, size):
                real, imag = block[k, r][0] * inverse, -block[k, r][1] * inverse
                rows[r], turned[r] = (
                    rows[r] - (real * rows[k] + imag * turned[k]),
                    turned[r] - (real * turned[k] - imag * rows[k]),
                )
                for j in range(r, size):
                    other = block[k, j]
                    block[r, j] = (
                        block[r, j][0] - (real * other[0] - imag * other[1]),
                        block[r, j][1] - (real * other[1] + imag * other[0]),
                    )
            for h in below:
                real, imag = cols[h, k][0] * inverse, cols[h, k][1] * inverse
                for j in range(k + 1, size):
                    other = block[k, j]
                    cols[h, j] = (
                        cols[h, j][0] - (real * other[0] - imag * other[1]),
                        cols[h, j][1] - (real * other[1] + imag * other[0]),
                    )
                step = real * rows[k] + imag * turned[k]
                new[h] = new[h] - (jnp.where(within >= o + size, step, 0.0) if h == g else step)
        kept = new.get(g, groups[g])
        for r in range(size):
            kept = jnp.where(within == o + r, rows[r], kept)
        for h in below:
            groups[h] = new[h]
        groups[g] = kept
    value = jnp.concatenate(groups, axis=0)
    pivot = jnp.sum(jnp.where(diagonal, value, 0.0), axis=1, keepdims=True)
    value = value * lax.rsqrt(pivot)
    second = jnp.where(lane >= 2 * WIDTH, value, 0.0)
    first = pltpu.roll(second, 2 * WIDTH, 1)
    turn_ref[0:WIDTH] = first
    turn_ref[WIDTH : 2 * WIDTH] = pair_swap(first)
    turn_ref[2 * WIDTH : 3 * WIDTH] = second
    turn_ref[3 * WIDTH :] = pair_swap(second)


def turn_kernel(wide_ref, turn_ref):
    packed = wide_ref[0, TILE:]
    for p in range(1, wide_ref.shape[0]):
        packed = packed + wide_ref[p, TILE:]
    packed = packed * (1.0 / IMAGES)
    value = jnp.concatenate([packed, pltpu.roll(packed, 2 * WIDTH, 1)], axis=0)
    invert_factor(jnp.where(lanes(value.shape) < 2 * WIDTH, value, 0.0), turn_ref)


def turn_of(wide):
    return pl.pallas_call(
        turn_kernel,
        out_shape=jax.ShapeDtypeStruct((TILE, TILE), jnp.float32),
        compiler_params=pltpu.CompilerParams(vmem_limit_bytes=6 * MIB),
        cost_estimate=pl.CostEstimate(flops=0, bytes_accessed=6 * MIB, transcendentals=0),
        name="turn",
    )(wide)


def basis_kernel(image_ref, gram_ref, out_ref, turn_ref):
    packed = jnp.sum(gram_ref[...], axis=0) * (1.0 / IMAGES)
    value = jnp.concatenate(
        [packed] + [pltpu.roll(packed, TILE - WIDTH * g, 1) for g in range(1, 4)], axis=0
    )
    across = jnp.concatenate([value] + [jnp.zeros_like(value)] * 3, axis=0).T[:WIDTH]
    lane = lanes(value.shape)
    row = lax.broadcasted_iota(jnp.int32, value.shape, 0)
    real = jnp.where(lane >= row, value, across)
    imag = jnp.where(lane == row, 0.0, jnp.where(lane < row, value, -across))
    value = jnp.where(lane < WIDTH, real, 0.0)
    value = value + jnp.where((lane >= WIDTH) & (lane < 2 * WIDTH), pltpu.roll(imag, WIDTH, 1), 0.0)
    invert_factor(value, turn_ref)
    out = nt_dot(image_ref[...], turn_ref[...]).T
    for part in range(2):
        for block in range(2):
            start = (2 * block + part) * WIDTH
            out_ref[part, :, block * TILE : (block + 1) * TILE] = out[start : start + WIDTH]


def last_basis(image, grams):
    return pl.pallas_call(
        basis_kernel,
        out_shape=jax.ShapeDtypeStruct((2, WIDTH, 2 * TILE), jnp.float32),
        scratch_shapes=[pltpu.VMEM((TILE, TILE), jnp.float32)],
        compiler_params=pltpu.CompilerParams(vmem_limit_bytes=6 * MIB),
        name="basis",
    )(image, grams)


def along_x(value, step):
    return lax.ppermute(value, "row", [(i, (i + 2 * step) % 8) for i in range(8)])


def other_core(value):
    return lax.ppermute(value, "row", [(i, i ^ 1) for i in range(8)])


def to_column(value):
    return lax.all_to_all(value, "col", split_axis=0, concat_axis=0, tiled=True)


def gather_row(value):
    mine = jnp.stack([value] + [along_x(value, d) for d in (1, 2, 3)], 0)
    return mine, other_core(mine)


def reduce_row(value):
    half = value.shape[0] // 2
    return scatter_x(value[:half], value[half:])


def scatter_x(own, other):
    mine = own + other_core(other)
    return [mine[0:1]] + [along_x(mine[d : d + 1], d) for d in (1, 2, 3)]


def shards(tile_weight, tile_angle, tile_list, tile_count, init_basis):
    place = lax.axis_index("row")
    x_place, core = place // 2, place % 2
    weights = tile_weight.reshape(SLOTS, TILE, TILE)
    angles = tile_angle.reshape(SLOTS, TILE, TILE)
    listing = tile_list.reshape(SLOTS, 2)
    row_of = listing[:, 0] % ROW_BLOCKS
    col_global = listing[:, 1]
    piece = col_global // ROW_BLOCKS
    core_away = (piece % 2) ^ core
    col_from = (core_away * 4 + (x_place - piece // 2) % 4) * 2 + col_global % 2
    col_to = (core_away * 4 + (piece // 2 - x_place) % 4) * 2 + col_global % 2
    live = (jnp.arange(2)[None, :] < tile_count.reshape(SLOTS // 2, 1)).reshape(SLOTS).astype(jnp.int32)
    slots = jnp.arange(SLOTS, dtype=jnp.int32)
    earlier = slots[None, :] < slots[:, None]
    count = jnp.sum(live)
    live_before = jnp.sum(jnp.where(earlier, live[None, :], 0), axis=1)
    at = jnp.where(live > 0, live_before, count + slots - live_before)
    code = slots + SLOTS * (col_from + COL_BLOCKS * (col_to + COL_BLOCKS * row_of))
    code = jnp.sum(jnp.where(at[None, :] == slots[:, None], code[None, :], 0), axis=1)
    order = code % SLOTS
    takes_col = code // SLOTS % COL_BLOCKS
    puts_col = code // (SLOTS * COL_BLOCKS) % COL_BLOCKS
    rows = code // (SLOTS * COL_BLOCKS * COL_BLOCKS)
    puts_col = jnp.where(slots < count, puts_col, COL_BLOCKS)
    rows = jnp.where(slots < count, rows, ROW_BLOCKS)
    count = count.reshape(1)

    plain, turned, row_part, own_part, other_part = complex_tiles(order, rows, puts_col, count, weights, angles)
    row_part = to_column(row_part)
    col_parts = scatter_x(own_part, other_part)
    basis = jnp.transpose(init_basis.reshape(2, WIDTH, 2, TILE), (3, 2, 0, 1)).reshape(TILE, TILE)
    scale, sent, spread_out = first_block(row_part, col_parts, basis)
    body, turn = None, None
    for rounds in range(ITERS):
        extra = 0 if body is None else WIDTH // 2
        near, far = gather_row(sent if body is None else body)
        column = to_column(spread_out)
        forward = products(
            1.0, takes_col, rows, count, plain, [near, far], (16, TILE + extra, TILE), True, "forward"
        )
        mirror = products(
            -1.0, rows, puts_col, count, turned, [column], (8, TILE, TILE), False, "mirror"
        )
        wide = to_column(forward)
        parts = reduce_row(mirror)
        if rounds > 0:
            turn = turn_of(wide)
        if rounds < ITERS - 1:
            body, spread_out = new_image(wide, parts, scale, turn, False)
        else:
            sent, gram = new_image(wide, parts, scale, turn, True)
    gram = gram + other_core(gram)
    grams = lax.all_to_all(
        jnp.broadcast_to(gram, (64, 8, TILE)),
        ("row", "col"),
        split_axis=0,
        concat_axis=0,
        tiled=True,
        axis_index_groups=[[16 * r + c for r in range(core, 8, 2) for c in range(16)] for core in (0, 1)],
    )
    return last_basis(sent, grams)


def solution(mesh):
    placed = (
        P(("row", "col"), None, None, None, None),
        P(("row", "col"), None, None, None, None),
        P(("row", "col"), None, None, None),
        P(("row", "col"), None),
        P(None, None, ("row", "col")),
    )
    return jax.shard_map(
        shards, mesh=mesh, in_specs=placed, out_specs=P(None, None, ("row", "col")), check_vma=False
    )
```

```python
import functools

import jax
import jax.numpy as jnp
from jax import lax
from jax.experimental import pallas as pl
from jax.experimental.pallas import tpu as pltpu
from jax.sharding import PartitionSpec as P

ITERS = 3
IMAGES = 32768
TILE = 128
WIDTH = 32
SLOTS = 256
ROW_BLOCKS = 32
COL_BLOCKS = 16
CHUNK = 16
TRIG_CHUNK = 16
HALF_SIN = (0.5, -0.020833322778344154, 0.00026040783268399537, -1.5475804957532091e-06, 5.088141019626846e-09)
HALF_COS = (0.9999999403953552, -0.1249997615814209, 0.0026039734948426485, -2.164632678613998e-05, 9.044046578310372e-08)
HIGHEST = lax.Precision.HIGHEST
MIB = 1 << 20


def horner(u, coefs):
    value = coefs[-1]
    for coef in coefs[-2::-1]:
        value = value * u + coef
    return value


def lanes(shape):
    return lax.broadcasted_iota(jnp.int32, shape, 1)


def pair_swap(x):
    even = (lanes(x.shape) // WIDTH) % 2 == 0
    return jnp.where(even, -pltpu.roll(x, TILE - WIDTH, 1), pltpu.roll(x, WIDTH, 1))


VECTOR = pl.BlockSpec(memory_space=pltpu.VMEM)
SCALAR = pl.BlockSpec(memory_space=pltpu.SMEM)


FAR = pl.BlockSpec(memory_space=pl.ANY)


def fetch(source, target, sems, c):
    part = pl.ds(c * CHUNK, CHUNK)
    return pltpu.make_async_copy(source.at[part], target.at[part], sems.at[c])


def start_fetches(source, target, sems, chunks):
    def start(c, carry):
        fetch(source, target, sems, c).start()
        return carry

    lax.fori_loop(0, chunks, start, 0)


def tiles_kernel(
    order, rows, cols, count, far_w, far_a, far_plain, far_turned, row_ref, own_ref, other_ref,
    w_ref, a_ref, plain, turned, row_acc, col_acc, w_sems, a_sems, out_sems,
):
    def start(c, carry):
        fetch(far_w, w_ref, w_sems, c).start()
        fetch(far_a, a_ref, a_sems, c).start()
        return carry

    lax.fori_loop(0, SLOTS // CHUNK, start, 0)
    row_acc[...] = jnp.zeros_like(row_acc)
    col_acc[...] = jnp.zeros_like(col_acc)
    chunks = pl.cdiv(count[0], CHUNK) * (CHUNK // TRIG_CHUNK)

    def outgoing(c):
        part = pl.ds(c * TRIG_CHUNK, TRIG_CHUNK)
        yield pltpu.make_async_copy(plain.at[c % 2], far_plain.at[part], out_sems.at[c % 2, 0])
        yield pltpu.make_async_copy(turned.at[c % 2], far_turned.at[part], out_sems.at[c % 2, 1])

    def arrive(c, carry):
        fetch(far_w, w_ref, w_sems, c).wait()
        fetch(far_a, a_ref, a_sems, c).wait()
        return carry

    def step(c, here):
        reach = order[c * TRIG_CHUNK + TRIG_CHUNK - 1] // CHUNK + 1
        need = jnp.where(c >= chunks - CHUNK // TRIG_CHUNK, SLOTS // CHUNK, reach)
        lax.fori_loop(here, need, arrive, 0)

        @pl.when(c >= 2)
        def _():
            for copy in outgoing(c - 2):
                copy.wait()

        side = c % 2
        for u in range(TRIG_CHUNK):
            slot = c * TRIG_CHUNK + u
            source = order[slot]
            theta = a_ref[source].astype(jnp.float32)
            w = w_ref[source].astype(jnp.float32)
            square = theta * theta
            sine = theta * horner(square, HALF_SIN)
            cosine = horner(square, HALF_COS)
            part = w * sine
            real = (0.5 * w - part * sine).astype(jnp.bfloat16)
            imag = (part * cosine).astype(jnp.bfloat16)
            plain[side, u, :, :TILE] = real
            plain[side, u, :, TILE:] = imag
            turned[side, u, :, :TILE] = real.T
            turned[side, u, :, TILE:] = imag.T
            row_acc[rows[slot]] += w
            col_acc[cols[slot]] += jnp.sum(w.reshape(TILE // 8, 8, TILE), axis=0)
        for copy in outgoing(c):
            copy.start()
        return need

    lax.fori_loop(0, chunks, step, 0)
    for p in range(ROW_BLOCKS // 2):
        sums = [jnp.sum(row_acc[2 * p + k].T, axis=0, keepdims=True) for k in range(2)]
        row_ref[p] = 0.5 * jnp.concatenate(sums * 4, axis=0)
    for p in range(COL_BLOCKS // 2):
        sums = [jnp.sum(col_acc[2 * p + k], axis=0, keepdims=True) for k in range(2)]
        col_ref = own_ref if p < 4 else other_ref
        col_ref[p % 4] = 0.5 * jnp.concatenate(sums * 4, axis=0)

    @pl.when(chunks >= 2)
    def _():
        for copy in outgoing(chunks - 2):
            copy.wait()

    for copy in outgoing(chunks - 1):
        copy.wait()


def complex_tiles(order, rows, cols, count, weights, angles):
    return pl.pallas_call(
        tiles_kernel,
        in_specs=[SCALAR] * 4 + [FAR, FAR],
        out_specs=[FAR, FAR, VECTOR, VECTOR, VECTOR],
        out_shape=[jax.ShapeDtypeStruct((SLOTS, TILE, 2 * TILE), jnp.bfloat16)] * 2
        + [
            jax.ShapeDtypeStruct((ROW_BLOCKS // 2, 8, TILE), jnp.float32),
            jax.ShapeDtypeStruct((COL_BLOCKS // 4, 8, TILE), jnp.float32),
            jax.ShapeDtypeStruct((COL_BLOCKS // 4, 8, TILE), jnp.float32),
        ],
        scratch_shapes=[
            pltpu.VMEM((SLOTS, TILE, TILE), jnp.bfloat16),
            pltpu.VMEM((SLOTS, TILE, TILE), jnp.bfloat16),
            pltpu.VMEM((2, TRIG_CHUNK, TILE, 2 * TILE), jnp.bfloat16),
            pltpu.VMEM((2, TRIG_CHUNK, TILE, 2 * TILE), jnp.bfloat16),
            pltpu.VMEM((ROW_BLOCKS + 1, TILE, TILE), jnp.float32),
            pltpu.VMEM((COL_BLOCKS + 1, 8, TILE), jnp.float32),
            pltpu.SemaphoreType.DMA((SLOTS // CHUNK,)),
            pltpu.SemaphoreType.DMA((SLOTS // CHUNK,)),
            pltpu.SemaphoreType.DMA((2, 2)),
        ],
        compiler_params=pltpu.CompilerParams(vmem_limit_bytes=58 * MIB),
        cost_estimate=pl.CostEstimate(flops=0, bytes_accessed=50 * MIB, transcendentals=0),
        name="complex_tiles",
    )(order, rows, cols, count, weights, angles)


def product_kernel(sign, sizes, apart, takes, puts, count, far_ref, *refs):
    x_refs = refs[: len(sizes)]
    out_ref, x_mat, acc, tiles_ref, sems = refs[len(sizes) :][:5]
    chunks = pl.cdiv(count[0], CHUNK)
    start_fetches(far_ref, tiles_ref, sems, chunks)
    low = lanes((TILE, TILE)) < 2 * WIDTH
    acc[...] = jnp.zeros_like(acc)
    x_mat[2 * sum(sizes)] = jnp.zeros_like(x_mat[0])
    base = 0
    for x_ref, size in zip(x_refs, sizes):
        for p in range(size):
            value = x_ref[p, :TILE].astype(jnp.float32)
            high = value.astype(jnp.bfloat16).astype(jnp.float32)
            rest = value - high
            for k in range(2):
                if k == 0:
                    top = jnp.where(low, high, pltpu.roll(rest, 2 * WIDTH, 1))
                else:
                    top = jnp.where(low, pltpu.roll(high, 2 * WIDTH, 1), rest)
                x_mat[base + 2 * p + k, :TILE] = top.astype(jnp.bfloat16)
                x_mat[base + 2 * p + k, TILE:] = (sign * pair_swap(top)).astype(jnp.bfloat16)
        base += 2 * size

    def add(c, size):
        for part in range(size):
            fetch(far_ref, tiles_ref, sems, c + part).wait()
        for u in range(CHUNK * size):
            slot = c * CHUNK + u
            acc[puts[slot]] += jnp.dot(
                tiles_ref[slot], x_mat[takes[slot]], preferred_element_type=jnp.float32
            )

    span = 2 if apart else 4

    def step(c, carry):
        add(span * c, span)
        return carry

    lax.fori_loop(0, chunks // span, step, 0)
    if span == 4:

        @pl.when(chunks % 4 >= 2)
        def _():
            add(chunks // 4 * 4, 2)


    @pl.when(chunks % 2 == 1)
    def _():
        add(chunks - 1, 1)

    near, out_sems = refs[len(sizes) :][5:] if apart else (out_ref, None)
    if out_ref.shape[1] > TILE:
        gram = sum(x_ref[p, TILE:] for x_ref, size in zip(x_refs, sizes) for p in range(size))
    copies = []
    for p in range(out_ref.shape[0]):
        if out_ref.shape[1] > TILE:
            near[p, TILE:] = gram
        first, second = acc[2 * p], acc[2 * p + 1]
        near[p, :TILE] = jnp.where(
            low,
            first + pltpu.roll(first, 2 * WIDTH, 1),
            second + pltpu.roll(second, 2 * WIDTH, 1),
        )
        if apart:
            copies.append(pltpu.make_async_copy(near.at[p], out_ref.at[p], out_sems.at[p]))
            copies[-1].start()
    for copy in copies:
        copy.wait()


def products(sign, takes, puts, count, tiles, sources, out_shape, apart, name):
    sizes = tuple(s.shape[0] for s in sources)
    scratch = [
        pltpu.VMEM((2 * sum(sizes) + 1, 2 * TILE, TILE), jnp.bfloat16),
        pltpu.VMEM((2 * out_shape[0] + 1, TILE, TILE), jnp.float32),
        pltpu.VMEM((SLOTS, TILE, 2 * TILE), jnp.bfloat16),
        pltpu.SemaphoreType.DMA((SLOTS // CHUNK,)),
    ]
    if apart:
        scratch += [pltpu.VMEM(out_shape, jnp.float32), pltpu.SemaphoreType.DMA((out_shape[0],))]
    return pl.pallas_call(
        functools.partial(product_kernel, sign, sizes, apart),
        in_specs=[SCALAR, SCALAR, SCALAR, FAR] + [VECTOR] * len(sources),
        out_specs=FAR if apart else VECTOR,
        scratch_shapes=scratch,
        out_shape=jax.ShapeDtypeStruct(out_shape, jnp.float32),
        compiler_params=pltpu.CompilerParams(vmem_limit_bytes=52 * MIB),
        cost_estimate=pl.CostEstimate(flops=0, bytes_accessed=30 * MIB, transcendentals=0),
        name=name,
    )(takes, puts, count, tiles, *sources)


def gather_kernel(turned, final, n_parts, *refs):
    wide_ref, part_refs = refs[0], refs[1 : 1 + n_parts]
    scale_ref = refs[1 + n_parts]
    rest = refs[2 + n_parts :]
    total = wide_ref[0, :TILE]
    for p in range(1, wide_ref.shape[0]):
        total = total + wide_ref[p, :TILE]
    for ref in part_refs:
        total = total + ref[0]
    scale = scale_ref[...]
    image = total * scale
    if turned:
        image = nt_dot(image, rest[0][...])
        rest = rest[1:]
    copies = []
    if not final:
        body_ref, far_ref, sems = rest
        body_ref[:TILE] = image * scale
        copies = spread_copies(body_ref.at[pl.ds(0, TILE)], far_ref, sems)
    across = image.T
    gram = nt_dot(across, across)
    pairs = gram[: 2 * WIDTH] + pltpu.roll(gram[2 * WIDTH :], 2 * WIDTH, 1)
    upper, lower = pairs[:WIDTH], pairs[WIDTH:]
    lane = lanes(upper.shape)
    other = jnp.where(lane < WIDTH, pltpu.roll(lower, TILE - WIDTH, 1), -pltpu.roll(lower, WIDTH, 1))
    both = upper + other
    if final:
        image_ref, gram_ref = rest
        image_ref[...] = image
        row = lax.broadcasted_iota(jnp.int32, upper.shape, 0)
        packed = jnp.where(lane >= row, both, pltpu.roll(both, TILE - WIDTH, 1))
        out = packed[:8]
        group = lanes((8, TILE)) // WIDTH
        for g in range(1, 4):
            out = jnp.where(group == g, pltpu.roll(packed[8 * g : 8 * g + 8], WIDTH * g, 1), out)
        gram_ref[0] = out
    else:
        low = lanes((WIDTH // 2, TILE)) < 2 * WIDTH
        body_ref[TILE:] = jnp.where(
            low, both[: WIDTH // 2], pltpu.roll(both[WIDTH // 2 :], 2 * WIDTH, 1)
        )
    for copy in copies:
        copy.wait()


def spread_copies(source, target, sems):
    copies = [pltpu.make_async_copy(source, target.at[p], sems.at[p]) for p in range(16)]
    for copy in copies:
        copy.start()
    return copies


def first_kernel(n_parts, *refs):
    wide_ref, part_refs = refs[0], refs[1 : 1 + n_parts]
    basis_ref, scale_ref, sent_ref, far_ref, sems = refs[1 + n_parts :]
    degree = wide_ref[0]
    for p in range(1, wide_ref.shape[0]):
        degree = degree + wide_ref[p]
    for ref in part_refs:
        degree = degree + ref[0]
    factor = lax.rsqrt(degree)
    row = lax.broadcasted_iota(jnp.int32, (TILE, TILE), 0)
    scale = jnp.where(row < 2 * WIDTH, factor[0:1], factor[1:2]).T
    scale_ref[...] = scale
    sent_ref[...] = (basis_ref[...] * scale).astype(jnp.bfloat16)
    for copy in spread_copies(sent_ref, far_ref, sems):
        copy.wait()


def first_block(wide, parts, basis):
    return pl.pallas_call(
        functools.partial(first_kernel, len(parts)),
        in_specs=[VECTOR] * (len(parts) + 2),
        out_specs=[VECTOR, VECTOR, FAR],
        out_shape=[
            jax.ShapeDtypeStruct((TILE, TILE), jnp.float32),
            jax.ShapeDtypeStruct((TILE, TILE), jnp.bfloat16),
            jax.ShapeDtypeStruct((16, TILE, TILE), jnp.bfloat16),
        ],
        scratch_shapes=[pltpu.SemaphoreType.DMA((16,))],
        compiler_params=pltpu.CompilerParams(vmem_limit_bytes=6 * MIB),
        cost_estimate=pl.CostEstimate(flops=0, bytes_accessed=6 * MIB, transcendentals=0),
        name="first_block",
    )(wide, *parts, basis)


def nt_dot(left, right):
    return lax.dot_general(
        left, right, (((1,), (1,)), ((), ())), precision=HIGHEST, preferred_element_type=jnp.float32
    )


def new_image(wide, parts, scale, turn, final):
    operands = [wide, *parts, scale] + ([] if turn is None else [turn])
    if final:
        shapes = [(TILE, TILE), (1, 8, TILE)]
    else:
        shapes = [(TILE + WIDTH // 2, TILE), (16, TILE, TILE)]
    return pl.pallas_call(
        functools.partial(gather_kernel, turn is not None, final, len(parts)),
        in_specs=[VECTOR] * len(operands),
        out_specs=[VECTOR, VECTOR if final else FAR],
        out_shape=[jax.ShapeDtypeStruct(shape, jnp.float32) for shape in shapes],
        scratch_shapes=[] if final else [pltpu.SemaphoreType.DMA((16,))],
        compiler_params=pltpu.CompilerParams(vmem_limit_bytes=6 * MIB),
        cost_estimate=pl.CostEstimate(flops=0, bytes_accessed=6 * MIB, transcendentals=0),
        name="new_image",
    )(*operands)


def spread(x, lane):
    return jnp.broadcast_to(x[:, lane : lane + 1], (8, TILE))


def invert_factor(value, turn_ref):
    size = 4
    lane = lanes((WIDTH, TILE))
    place = lax.broadcasted_iota(jnp.int32, (WIDTH, TILE), 0)
    diagonal = lane == place
    trace = jnp.sum(jnp.where(diagonal, value, 0.0))
    ridge = 0.01 * trace / WIDTH + 1e-6
    value = value + jnp.where(diagonal, ridge, 0.0)
    value = value + jnp.where(lane == place + 2 * WIDTH, 1.0, 0.0)
    groups = [value[8 * g : 8 * g + 8] for g in range(4)]
    within = lax.broadcasted_iota(jnp.int32, (8, TILE), 0)
    for c in range(0, WIDTH, size):
        g, o = c // 8, c % 8
        rows = [jnp.broadcast_to(groups[g][o + r : o + r + 1], (8, TILE)) for r in range(size)]
        turned = [pair_swap(row) for row in rows]
        block = {
            (r, k): (spread(rows[r], c + k), spread(rows[r], WIDTH + c + k))
            for r in range(size)
            for k in range(r, size)
        }
        below = list(range(g if o + size < 8 else g + 1, 4))
        cols = {
            (h, k): (spread(groups[h], c + k), spread(groups[h], WIDTH + c + k))
            for h in below
            for k in range(size)
        }
        new = {h: groups[h] for h in below}
        for k in range(size):
            inverse = 1.0 / block[k, k][0]
            for r in range(k + 1, size):
                real, imag = block[k, r][0] * inverse, -block[k, r][1] * inverse
                rows[r], turned[r] = (
                    rows[r] - (real * rows[k] + imag * turned[k]),
                    turned[r] - (real * turned[k] - imag * rows[k]),
                )
                for j in range(r, size):
                    other = block[k, j]
                    block[r, j] = (
                        block[r, j][0] - (real * other[0] - imag * other[1]),
                        block[r, j][1] - (real * other[1] + imag * other[0]),
                    )
            for h in below:
                real, imag = cols[h, k][0] * inverse, cols[h, k][1] * inverse
                for j in range(k + 1, size):
                    other = block[k, j]
                    cols[h, j] = (
                        cols[h, j][0] - (real * other[0] - imag * other[1]),
                        cols[h, j][1] - (real * other[1] + imag * other[0]),
                    )
                step = real * rows[k] + imag * turned[k]
                new[h] = new[h] - (jnp.where(within >= o + size, step, 0.0) if h == g else step)
        kept = new.get(g, groups[g])
        for r in range(size):
            kept = jnp.where(within == o + r, rows[r], kept)
        for h in below:
            groups[h] = new[h]
        groups[g] = kept
    value = jnp.concatenate(groups, axis=0)
    pivot = jnp.sum(jnp.where(diagonal, value, 0.0), axis=1, keepdims=True)
    value = value * lax.rsqrt(pivot)
    second = jnp.where(lane >= 2 * WIDTH, value, 0.0)
    first = pltpu.roll(second, 2 * WIDTH, 1)
    turn_ref[0:WIDTH] = first
    turn_ref[WIDTH : 2 * WIDTH] = pair_swap(first)
    turn_ref[2 * WIDTH : 3 * WIDTH] = second
    turn_ref[3 * WIDTH :] = pair_swap(second)


def turn_kernel(wide_ref, turn_ref):
    packed = wide_ref[0, TILE:]
    for p in range(1, wide_ref.shape[0]):
        packed = packed + wide_ref[p, TILE:]
    packed = packed * (1.0 / IMAGES)
    value = jnp.concatenate([packed, pltpu.roll(packed, 2 * WIDTH, 1)], axis=0)
    invert_factor(jnp.where(lanes(value.shape) < 2 * WIDTH, value, 0.0), turn_ref)


def turn_of(wide):
    return pl.pallas_call(
        turn_kernel,
        out_shape=jax.ShapeDtypeStruct((TILE, TILE), jnp.float32),
        compiler_params=pltpu.CompilerParams(vmem_limit_bytes=6 * MIB),
        cost_estimate=pl.CostEstimate(flops=0, bytes_accessed=6 * MIB, transcendentals=0),
        name="turn",
    )(wide)


def basis_kernel(image_ref, gram_ref, out_ref, turn_ref):
    packed = jnp.sum(gram_ref[...], axis=0) * (1.0 / IMAGES)
    value = jnp.concatenate(
        [packed] + [pltpu.roll(packed, TILE - WIDTH * g, 1) for g in range(1, 4)], axis=0
    )
    across = jnp.concatenate([value] + [jnp.zeros_like(value)] * 3, axis=0).T[:WIDTH]
    lane = lanes(value.shape)
    row = lax.broadcasted_iota(jnp.int32, value.shape, 0)
    real = jnp.where(lane >= row, value, across)
    imag = jnp.where(lane == row, 0.0, jnp.where(lane < row, value, -across))
    value = jnp.where(lane < WIDTH, real, 0.0)
    value = value + jnp.where((lane >= WIDTH) & (lane < 2 * WIDTH), pltpu.roll(imag, WIDTH, 1), 0.0)
    invert_factor(value, turn_ref)
    out = nt_dot(image_ref[...], turn_ref[...]).T
    for part in range(2):
        for block in range(2):
            start = (2 * block + part) * WIDTH
            out_ref[part, :, block * TILE : (block + 1) * TILE] = out[start : start + WIDTH]


def last_basis(image, grams):
    return pl.pallas_call(
        basis_kernel,
        out_shape=jax.ShapeDtypeStruct((2, WIDTH, 2 * TILE), jnp.float32),
        scratch_shapes=[pltpu.VMEM((TILE, TILE), jnp.float32)],
        compiler_params=pltpu.CompilerParams(vmem_limit_bytes=6 * MIB),
        name="basis",
    )(image, grams)


def along_x(value, step):
    return lax.ppermute(value, "row", [(i, (i + 2 * step) % 8) for i in range(8)])


def other_core(value):
    return lax.ppermute(value, "row", [(i, i ^ 1) for i in range(8)])


def to_column(value):
    return lax.all_to_all(value, "col", split_axis=0, concat_axis=0, tiled=True)


def gather_row(value):
    mine = jnp.stack([value] + [along_x(value, d) for d in (1, 2, 3)], 0)
    return mine, other_core(mine)


def reduce_row(value):
    half = value.shape[0] // 2
    return scatter_x(value[:half], value[half:])


def scatter_x(own, other):
    mine = own + other_core(other)
    return [mine[0:1]] + [along_x(mine[d : d + 1], d) for d in (1, 2, 3)]


def shards(tile_weight, tile_angle, tile_list, tile_count, init_basis):
    place = lax.axis_index("row")
    x_place, core = place // 2, place % 2
    weights = tile_weight.reshape(SLOTS, TILE, TILE)
    angles = tile_angle.reshape(SLOTS, TILE, TILE)
    listing = tile_list.reshape(SLOTS, 2)
    row_of = listing[:, 0] % ROW_BLOCKS
    col_global = listing[:, 1]
    piece = col_global // ROW_BLOCKS
    core_away = (piece % 2) ^ core
    col_from = (core_away * 4 + (x_place - piece // 2) % 4) * 2 + col_global % 2
    col_to = (core_away * 4 + (piece // 2 - x_place) % 4) * 2 + col_global % 2
    live = (jnp.arange(2)[None, :] < tile_count.reshape(SLOTS // 2, 1)).reshape(SLOTS).astype(jnp.int32)
    slots = jnp.arange(SLOTS, dtype=jnp.int32)
    earlier = slots[None, :] < slots[:, None]
    count = jnp.sum(live)
    live_before = jnp.sum(jnp.where(earlier, live[None, :], 0), axis=1)
    at = jnp.where(live > 0, live_before, count + slots - live_before)
    code = slots + SLOTS * (col_from + COL_BLOCKS * (col_to + COL_BLOCKS * row_of))
    code = jnp.sum(jnp.where(at[None, :] == slots[:, None], code[None, :], 0), axis=1)
    order = code % SLOTS
    takes_col = code // SLOTS % COL_BLOCKS
    puts_col = code // (SLOTS * COL_BLOCKS) % COL_BLOCKS
    rows = code // (SLOTS * COL_BLOCKS * COL_BLOCKS)
    puts_col = jnp.where(slots < count, puts_col, COL_BLOCKS)
    rows = jnp.where(slots < count, rows, ROW_BLOCKS)
    count = count.reshape(1)

    plain, turned, row_part, own_part, other_part = complex_tiles(order, rows, puts_col, count, weights, angles)
    row_part = to_column(row_part)
    col_parts = scatter_x(own_part, other_part)
    basis = jnp.transpose(init_basis.reshape(2, WIDTH, 2, TILE), (3, 2, 0, 1)).reshape(TILE, TILE)
    scale, sent, spread_out = first_block(row_part, col_parts, basis)
    body, turn = None, None
    for rounds in range(ITERS):
        extra = 0 if body is None else WIDTH // 2
        near, far = gather_row(sent if body is None else body)
        column = to_column(spread_out)
        forward = products(
            1.0, takes_col, rows, count, plain, [near, far], (16, TILE + extra, TILE), True, "forward"
        )
        mirror = products(
            -1.0, rows, puts_col, count, turned, [column], (8, TILE, TILE), False, "mirror"
        )
        wide = to_column(forward)
        parts = reduce_row(mirror)
        if rounds > 0:
            turn = turn_of(wide)
        if rounds < ITERS - 1:
            body, spread_out = new_image(wide, parts, scale, turn, False)
        else:
            sent, gram = new_image(wide, parts, scale, turn, True)
    gram = gram + other_core(gram)
    grams = lax.all_to_all(
        jnp.broadcast_to(gram, (64, 8, TILE)),
        ("row", "col"),
        split_axis=0,
        concat_axis=0,
        tiled=True,
        axis_index_groups=[[16 * r + c for r in range(core, 8, 2) for c in range(16)] for core in (0, 1)],
    )
    return last_basis(sent, grams)


def solution(mesh):
    placed = (
        P(("row", "col"), None, None, None, None),
        P(("row", "col"), None, None, None, None),
        P(("row", "col"), None, None, None),
        P(("row", "col"), None),
        P(None, None, ("row", "col")),
    )
    return jax.shard_map(
        shards, mesh=mesh, in_specs=placed, out_specs=P(None, None, ("row", "col")), check_vma=False
    )
```
